128 devices in a mesh: seq: 16 (over y, z), head: 8 (over x, core).
Axes of the slice: x: 4, y: 4, z: 4, core: 2. Of those that a mesh axis runs over, the one named last changes fastest.
Arguments:
- modulation: bfloat16 [16384, 4608], P(('seq', 'head')), may hold values from -3 to 3
- latents: bfloat16 [16384, 16], P(('seq', 'head')), may hold values from -6 to 6
- noise: bfloat16 [16384, 64], P(('seq', 'head')), may hold values from -6 to 6
- times: bfloat16 [16384, 4], P(('seq', 'head')), may hold values from 0.019897461 to 0.9765625
- image_rows: int32 [128], P(('seq', 'head')), may hold values from 1 to 128, 8192 in all
- in_weight: bfloat16 [16, 1536], replicated, may hold values from -1.5 to 1.5
- fc1_weight: bfloat16 [1536, 1536], replicated, may hold values from -0.15625 to 0.15625
- fc2_weight: bfloat16 [1536, 1536], replicated, may hold values from -0.15625 to 0.15625
- out_weight: bfloat16 [16, 1536], replicated, may hold values from -0.15625 to 0.15625
Outputs:
- mod_grad: float32 [16384, 4608], P(('seq', 'head'))
- fc1_grad: float32 [1536, 1536], P(('seq', 'head'))
- fc2_grad: float32 [1536, 1536], P(('seq', 'head'))
- in_grad: float32 [16, 1536], P(None, ('seq', 'head'))
- out_grad: float32 [16, 1536], P(None, ('seq', 'head'))
The draws below stay inside these ranges and needn't reach their ends.
Inputs may be any that keep to these rules, and one draw needn't show every extreme that they name: `image_rows`: the counts sum to exactly 8192; a device's image tokens are its first rows.
All inputs are finite; a program needn't handle non-finite values.
Results may differ from the reference program's by a relative error of at most 0.005.
The reference program's roundings to bfloat16 on the way count: a program that leaves them out, or rounds other values in their place, can miss the bound.
Values may be sent and summed in bfloat16 or wider, within the bound.
A program may use at most 128 MiB of HBM per device.

```python
import math
import jax
import jax.numpy as jnp
import numpy as np
from jax import lax

W = 1536
C = 16
DRAWS = 4
ROWS = 128
TOKENS = 16384
IMG_TOTAL = 8192
DEVICES = 128


def block_scale(own_key, extent, split, low, high):
    level, own = 1.0, jax.random.fold_in(own_key, 6)
    for axis_at, shards_of in split:
        draws = jnp.exp(jax.random.uniform(jax.random.fold_in(own, axis_at), (shards_of,), jnp.float32, low / len(split), high / len(split)))
        level = level * jnp.repeat(draws, extent[axis_at] // shards_of).reshape([-1 if axis == axis_at else 1 for axis in range(len(extent))])
    return level


def split_up(amount, total, reach, slope):
    weights = [(1 << 20) // math.isqrt(rank ** slope) + 1 for rank in range(2, amount + 1)]
    spare, given = total - reach - (amount - 1), [1] * (amount - 1)
    while spare > 0:
        candidates = [i for i in range(amount - 1) if given[i] < reach]
        pool, remaining = sum([weights[i] for i in candidates]), spare
        for i in candidates:
            extra = min(reach - given[i], max(1, remaining * weights[i] // pool), spare)
            given[i] = given[i] + extra
            spare = spare - extra
    return np.array([reach] + given)


def uneven(rng, number_of, total, most, slope):
    if number_of == 2:
        one = jax.random.randint(rng, (), max(1, total - most), min(most, total - 1) + 1)
        return jnp.stack([one, total - one])
    lengths = jnp.asarray(split_up(number_of, total, most, slope), jnp.int32)
    pairs = (number_of - 1) // 2
    giver, receiver = lengths[1:1 + 2 * pairs:2], lengths[2:2 + 2 * pairs:2]
    slack = jnp.minimum(giver - 1, most - receiver)
    passed = jax.random.randint(jax.random.fold_in(rng, 1), (pairs,), 0, 1 << 20) % (slack + 1)
    lengths = lengths.at[1:1 + 2 * pairs:2].set(giver - passed).at[2:2 + 2 * pairs:2].set(receiver + passed)
    return lengths[jax.random.permutation(jax.random.fold_in(rng, 2), number_of)]


def scatter_about(rng, shape, width, limit, cuts=(), held_as=jnp.bfloat16):
    array = width * jax.random.normal(rng, shape, jnp.float32)
    if cuts:
        array = array * block_scale(rng, shape, cuts, -0.22, 0.18)
    return jnp.clip(array, -limit, limit).astype(held_as)


def setup_inputs(seed: int = 0) -> dict:
    key_of = jax.random.split(jax.random.key(seed), 10)
    modulation = scatter_about(key_of[0], (TOKENS, 3 * W), 0.5, 3.0, ((0, 128),))
    latents = scatter_about(key_of[1], (TOKENS, C), 1.0, 6.0, ((0, 128),))
    noise = scatter_about(key_of[2], (TOKENS, DRAWS * C), 1.0, 6.0, ((0, 128),))
    times = jnp.clip(0.019897461 + 0.95666504 * jax.random.uniform(key_of[3], (TOKENS, DRAWS), jnp.float32) ** block_scale(key_of[3], (TOKENS, DRAWS), ((0, 128),), -0.2, 0.2), 0.019897461, 0.9765625).astype(jnp.bfloat16)
    image_rows = uneven(key_of[4], DEVICES, IMG_TOTAL, ROWS, 2).astype(jnp.int32)
    in_weight = scatter_about(key_of[5], (C, W), C ** -0.5, 1.5)
    fc1_weight = scatter_about(key_of[6], (W, W), W ** -0.5, 0.15625)
    fc2_weight = scatter_about(key_of[7], (W, W), W ** -0.5, 0.15625)
    out_weight = scatter_about(key_of[8], (C, W), W ** -0.5, 0.15625)
    return {"modulation": modulation, "latents": latents, "noise": noise, "times": times, "image_rows": image_rows, "in_weight": in_weight, "fc1_weight": fc1_weight, "fc2_weight": fc2_weight, "out_weight": out_weight}


norm_eps = 1e-06

def layer_norm(stream):
    center = stream - lax.optimization_barrier(jnp.mean(stream, axis=-1, keepdims=True))
    rstd_val = lax.rsqrt(lax.optimization_barrier(jnp.mean(center * center, axis=-1, keepdims=True)) + norm_eps)
    return (center * rstd_val, rstd_val)

def norm_backward(grad_in, normed, rstd_val):
    return rstd_val * (grad_in - lax.optimization_barrier(jnp.mean(grad_in, axis=-1, keepdims=True)) - normed * lax.optimization_barrier(jnp.mean(grad_in * normed, axis=-1, keepdims=True)))

def contract_rows(left_rows, right_rows):
    return lax.dot_general(left_rows, right_rows, (((0,), (0,)), ((), ())), preferred_element_type=jnp.float32)

def head_pass(modulation, latents, noise, times, live_mask, in_weight, fc1_weight, fc2_weight, out_weight):
    token_count = modulation.shape[0]
    model_width = in_weight.shape[1]
    channel_count = in_weight.shape[0]
    draw_count = times.shape[1]
    mod_values = modulation.astype(jnp.float32)
    shift_part = mod_values[:, :model_width]
    scale_plus = 1.0 + mod_values[:, model_width:2 * model_width]
    gate_part = mod_values[:, 2 * model_width:]
    noise_draw = noise.astype(jnp.float32).reshape(token_count, draw_count, channel_count).transpose(1, 0, 2)
    angles = 0.5 * jnp.pi * jnp.transpose(times.astype(jnp.float32))[:, :, None]
    noisy_in = (jnp.cos(angles) * latents.astype(jnp.float32)[None] + jnp.sin(angles) * noise_draw).astype(jnp.bfloat16)
    noisy_flat = noisy_in.reshape(draw_count * token_count, channel_count)
    stream_in = jnp.dot(noisy_flat, in_weight, preferred_element_type=jnp.float32).reshape(draw_count, token_count, model_width)
    normed_in, rstd_in = layer_norm(stream_in)
    block_in = (normed_in * scale_plus + shift_part).astype(jnp.bfloat16).reshape(-1, model_width)
    hidden_pre = jnp.dot(block_in, fc1_weight, preferred_element_type=jnp.float32)
    sigmoid_hid = jax.nn.sigmoid(hidden_pre)
    hidden_act = (hidden_pre * sigmoid_hid).astype(jnp.bfloat16)
    branch_out = jnp.dot(hidden_act, fc2_weight, preferred_element_type=jnp.float32).reshape(draw_count, token_count, model_width)
    stream_out = stream_in + gate_part * branch_out
    normed_out, rstd_out = layer_norm(stream_out)
    final_in = normed_out.astype(jnp.bfloat16).reshape(-1, model_width)
    predicted = jnp.dot(final_in, out_weight.T, preferred_element_type=jnp.float32).reshape(draw_count, token_count, channel_count)
    pred_grad = (2.0 * (predicted - noise_draw) * live_mask[None, :, None]).astype(jnp.bfloat16).reshape(-1, channel_count)
    final_grad = jnp.dot(pred_grad, out_weight, preferred_element_type=jnp.float32).reshape(draw_count, token_count, model_width)
    stream_grad = norm_backward(final_grad, normed_out, rstd_out)
    branch_grad = (stream_grad * gate_part).astype(jnp.bfloat16).reshape(-1, model_width)
    act_grad = jnp.dot(branch_grad, fc2_weight.T, preferred_element_type=jnp.float32)
    pre_grad = (act_grad * sigmoid_hid * (1.0 + hidden_pre * (1.0 - sigmoid_hid))).astype(jnp.bfloat16)
    block_grad = jnp.dot(pre_grad, fc1_weight.T, preferred_element_type=jnp.float32).reshape(draw_count, token_count, model_width)
    input_grad = stream_grad + norm_backward(block_grad * scale_plus, normed_in, rstd_in)
    input_bf = input_grad.astype(jnp.bfloat16).reshape(-1, model_width)
    mod_grad = jnp.concatenate([lax.optimization_barrier(jnp.sum(block_grad, axis=0)), lax.optimization_barrier(jnp.sum(block_grad * normed_in, axis=0)), lax.optimization_barrier(jnp.sum(stream_grad * branch_out, axis=0))], axis=-1)
    return (mod_grad, (block_in, pre_grad, hidden_act, branch_grad, noisy_flat, input_bf, pred_grad, final_in))

def reference(modulation, latents, noise, times, image_rows, in_weight, fc1_weight, fc2_weight, out_weight):
    block_count = image_rows.shape[0]
    model_width = in_weight.shape[1]
    channel_count = in_weight.shape[0]

    def block_step(totals, block_args):
        mod_block, lat_block, noise_block, time_block, live_count = block_args
        live_mask = (jnp.arange(ROWS) < live_count).astype(jnp.float32)
        mod_grad, pieces = head_pass(mod_block, lat_block, noise_block, time_block, live_mask, in_weight, fc1_weight, fc2_weight, out_weight)
        block_in, pre_grad, hidden_act, branch_grad, noisy_flat, input_bf, pred_grad, final_in = pieces
        totals = (totals[0] + contract_rows(block_in, pre_grad), totals[1] + contract_rows(hidden_act, branch_grad), totals[2] + contract_rows(noisy_flat, input_bf), totals[3] + contract_rows(pred_grad, final_in))
        return (totals, mod_grad)
    init_totals = (jnp.zeros((model_width, model_width), jnp.float32), jnp.zeros((model_width, model_width), jnp.float32), jnp.zeros((channel_count, model_width), jnp.float32), jnp.zeros((channel_count, model_width), jnp.float32))
    stacked = (modulation.reshape(block_count, ROWS, -1), latents.reshape(block_count, ROWS, -1), noise.reshape(block_count, ROWS, -1), times.reshape(block_count, ROWS, -1), image_rows)
    totals, mod_grads = lax.scan(block_step, init_totals, stacked)
    factor = IMG_TOTAL ** (-0.5)
    return (mod_grads.reshape(TOKENS, 3 * model_width), totals[0] * factor, totals[1] * factor, totals[2] * factor, totals[3] * factor)
```

```python
import jax
import jax.numpy as jnp
from jax import lax
from jax.experimental import pallas as pl
from jax.experimental.pallas import tpu as pltpu
from jax.sharding import PartitionSpec as P

f32, bf16 = jnp.float32, jnp.bfloat16
EPS = 1e-6
W, C, DRAWS, ROWS, NB = 1536, 16, 4, 128, 256
R = DRAWS * ROWS
NT = (((1,), (1,)), ((), ()))
TN = (((0,), (0,)), ((), ()))


def dot(a, b):
    return jnp.dot(a, b, preferred_element_type=f32)


def dot_nt(a, b):
    return lax.dot_general(a, b, NT, preferred_element_type=f32)


def dot_tn(a, b):
    return lax.dot_general(a, b, TN, preferred_element_type=f32)


def columns(j, base=0):
    return pl.ds(pl.multiple_of(base + j * NB, NB), NB)


def make_noisy(lat, noise, times, noisy_s, nd_s):
    ang = (0.5 * jnp.pi) * times[...].astype(f32)
    cosv, sinv = jnp.cos(ang), jnp.sin(ang)
    latv = lat[...].astype(f32)
    for k in range(DRAWS):
        nz = noise[:, C * k:C * (k + 1)].astype(f32)
        noisy_s[k * ROWS:(k + 1) * ROWS, :] = (cosv[:, k:k + 1] * latv + sinv[:, k:k + 1] * nz).astype(bf16)
        nd_s[k * ROWS:(k + 1) * ROWS, :] = nz


def stream(noisy_s, inw, st_s):
    @pl.loop(0, W // NB)
    def _(j):
        st_s[:, columns(j)] = dot(noisy_s[...], inw[:, columns(j)])


def norm_in(mod, st_s, ni_s, ri_s, bi_s):
    @pl.loop(0, ROWS // 16)
    def _(i):
        t0 = pl.multiple_of(i * 16, 16)
        t = pl.ds(t0, 16)
        for k in range(DRAWS):
            r = pl.ds(pl.multiple_of(k * ROWS + t0, 16), 16)
            x = st_s[r, :]
            c = x - jnp.mean(x, axis=-1, keepdims=True)
            rs = lax.rsqrt(jnp.mean(c * c, axis=-1, keepdims=True) + EPS)
            n = c * rs
            ni_s[r, :] = n
            ri_s[r, :] = rs
            bi_s[r, :] = (n * (1.0 + mod[t, W:2 * W].astype(f32)) + mod[t, 0:W].astype(f32)).astype(bf16)


def fc1_fwd(bi_s, fc1, h_s, d_s):
    @pl.loop(0, W // NB)
    def _(j):
        hp = dot(bi_s[...], fc1[:, columns(j)])
        sg = jax.nn.sigmoid(hp)
        h_s[:, columns(j)] = (hp * sg).astype(bf16)
        d_s[:, columns(j)] = sg * (1.0 + hp * (1.0 - sg))


def fc2_fwd(mod, h_s, fc2, st_s, bo_s):
    @pl.loop(0, W // NB)
    def _(j):
        bo = dot(h_s[...], fc2[:, columns(j)])
        bo_s[:, columns(j)] = bo
        gate = mod[:, columns(j, 2 * W)].astype(f32)
        for k in range(DRAWS):
            r = slice(k * ROWS, (k + 1) * ROWS)
            st_s[r, columns(j)] = st_s[r, columns(j)] + gate * bo[r]


def norm_out(st_s, ro_s, fin_s):
    @pl.loop(0, R // 32)
    def _(i):
        r = pl.ds(pl.multiple_of(i * 32, 32), 32)
        x = st_s[r, :]
        c = x - jnp.mean(x, axis=-1, keepdims=True)
        rs = lax.rsqrt(jnp.mean(c * c, axis=-1, keepdims=True) + EPS)
        n = c * rs
        st_s[r, :] = n
        ro_s[r, :] = rs
        fin_s[r, :] = n.astype(bf16)


def predict(cnt, fin_s, outw, nd_s, pd_s, m1_s, m2_s):
    pred = dot_nt(fin_s[...], outw[...])
    ows = dot_nt(jnp.ones((8, W), bf16), outw[...])[0:1, :] * (1.0 / W)
    tok = lax.broadcasted_iota(jnp.int32, (R, 1), 0) & (ROWS - 1)
    live = (tok < cnt[0]).astype(f32)
    pd = (2.0 * (pred - nd_s[...]) * live).astype(bf16)
    pd_s[...] = pd
    pf = pd.astype(f32)
    m1_s[...] = jnp.sum(pf * ows, axis=-1, keepdims=True)
    m2_s[...] = jnp.sum(pf * pred, axis=-1, keepdims=True) * (1.0 / W)


def stream_grad(mod, pd_s, outw, st_s, ro_s, m1_s, m2_s, bo_s, sg_s, bg_s, mod_out):
    @pl.loop(0, W // NB)
    def _(j):
        fg = dot(pd_s[...], outw[:, columns(j)])
        gate = mod[:, columns(j, 2 * W)].astype(f32)
        acc = None
        for k in range(DRAWS):
            r = slice(k * ROWS, (k + 1) * ROWS)
            sg = ro_s[r, :] * (fg[r] - m1_s[r, :] - st_s[r, columns(j)] * m2_s[r, :])
            sg_s[r, columns(j)] = sg
            bg_s[r, columns(j)] = (sg * gate).astype(bf16)
            t = sg * bo_s[r, columns(j)]
            acc = t if acc is None else acc + t
        mod_out[:, columns(j, 2 * W)] = acc


def pre_grad(bg_s, fc2, d_s, pg_s):
    @pl.loop(0, W // NB)
    def _(j):
        ag = dot_nt(bg_s[...], fc2[columns(j), :])
        pg_s[:, columns(j)] = (ag * d_s[:, columns(j)]).astype(bf16)


def block_grad(mod, pg_s, fc1, ni_s, blk_s, a1_s, a2_s, mod_out):
    a1_s[...] = jnp.zeros_like(a1_s)
    a2_s[...] = jnp.zeros_like(a2_s)

    @pl.loop(0, W // NB)
    def _(j):
        blk = dot_nt(pg_s[...], fc1[columns(j), :])
        sp = 1.0 + mod[:, columns(j, W)].astype(f32)
        s0 = s1 = None
        for k in range(DRAWS):
            r = slice(k * ROWS, (k + 1) * ROWS)
            n = ni_s[r, columns(j)]
            b = blk[r]
            bn = b * n
            g = b * sp
            blk_s[r, columns(j)] = g
            gn = g * n
            a1_s[r, :] = a1_s[r, :] + (g[:, :128] + g[:, 128:])
            a2_s[r, :] = a2_s[r, :] + (gn[:, :128] + gn[:, 128:])
            s0 = b if s0 is None else s0 + b
            s1 = bn if s1 is None else s1 + bn
        mod_out[:, columns(j)] = s0
        mod_out[:, columns(j, W)] = s1


def input_grad(ri_s, ni_s, sg_s, blk_s, a1_s, a2_s, ib_s):
    a1_s[:, 0:1] = jnp.sum(a1_s[...], axis=-1, keepdims=True) * (1.0 / W)
    a2_s[:, 0:1] = jnp.sum(a2_s[...], axis=-1, keepdims=True) * (1.0 / W)

    @pl.loop(0, R // 32)
    def _(i):
        r = pl.ds(pl.multiple_of(i * 32, 32), 32)
        v = sg_s[r, :] + ri_s[r, :] * (blk_s[r, :] - a1_s[r, 0:1] - ni_s[r, :] * a2_s[r, 0:1])
        ib_s[r, :] = v.astype(bf16)


def edges(noisy_s, ib_s, pd_s, fin_s, e_out):
    e_out[0:C, :] = dot_tn(noisy_s[...], ib_s[...])
    e_out[C:2 * C, :] = dot_tn(pd_s[...], fin_s[...])


def local_kernel(cnt, mod, lat, noise, times, inw, fc1, fc2, outw,
                 mod_out, h_s, bg_s, bi_s, pg_s, e_out,
                 noisy_s, nd_s, st_s, ni_s, ri_s, d_s, bo_s, ro_s, fin_s, pd_s, m1_s, m2_s,
                 sg_s, blk_s, a1_s, a2_s, ib_s):
    make_noisy(lat, noise, times, noisy_s, nd_s)
    stream(noisy_s, inw, st_s)
    norm_in(mod, st_s, ni_s, ri_s, bi_s)
    fc1_fwd(bi_s, fc1, h_s, d_s)
    fc2_fwd(mod, h_s, fc2, st_s, bo_s)
    norm_out(st_s, ro_s, fin_s)
    predict(cnt, fin_s, outw, nd_s, pd_s, m1_s, m2_s)
    stream_grad(mod, pd_s, outw, st_s, ro_s, m1_s, m2_s, bo_s, sg_s, bg_s, mod_out)
    pre_grad(bg_s, fc2, d_s, pg_s)
    block_grad(mod, pg_s, fc1, ni_s, blk_s, a1_s, a2_s, mod_out)
    input_grad(ri_s, ni_s, sg_s, blk_s, a1_s, a2_s, ib_s)
    edges(noisy_s, ib_s, pd_s, fin_s, e_out)


def local_call(mod, lat, noise, times, cnt, inw, fc1, fc2, outw):
    v = pl.BlockSpec(memory_space=pltpu.VMEM)
    S = lambda s, d=f32: pltpu.VMEM(s, d)
    O = jax.ShapeDtypeStruct
    return pl.pallas_call(
        local_kernel,
        out_shape=[O((ROWS, 3 * W), f32)] + [O((R, W), bf16)] * 4 + [O((2 * C, W), f32)],
        in_specs=[pl.BlockSpec(memory_space=pltpu.SMEM)] + [v] * 8,
        out_specs=[v] * 6,
        scratch_shapes=[S((R, C), bf16), S((R, C)), S((R, W)), S((R, W)), S((R, 1)), S((R, W)), S((R, W)), S((R, 1)),
                        S((R, W), bf16), S((R, C), bf16), S((R, 1)), S((R, 1)), S((R, W)), S((R, W)), S((R, 128)),
                        S((R, 128)), S((R, W), bf16)],
        compiler_params=pltpu.CompilerParams(vmem_limit_bytes=60 * 1024 * 1024),
        cost_estimate=pl.CostEstimate(flops=8 * R * W * W, bytes_accessed=20_000_000, transcendentals=R * W),
    )(cnt, mod, lat, noise, times, inw, fc1, fc2, outw)


MESH = pl.DeviceIdType.MESH
ORDER = (("y", "z", "x"), ("z", "x", "y"), ("x", "y", "z"))
HALF, PART, PIECE = W // 2, W // 6, 24
FACTOR = (ROWS * 128 // 2) ** -0.5


def place():
    s, h = lax.axis_index("seq"), lax.axis_index("head")
    return {"y": lax.div(s, 4), "z": lax.rem(s, 4), "x": lax.div(h, 2)}, lax.rem(h, 2)


def away(pos, axis, d):
    out = dict(pos)
    out[axis] = lax.rem(pos[axis] + d, 4)
    return out


def device(pos, core):
    return (pos["y"] * 4 + pos["z"], pos["x"] * 2 + core)


def remote(src, dst, ssem, rsem, dev):
    return pltpu.make_async_remote_copy(
        src_ref=src, dst_ref=dst, send_sem=ssem, recv_sem=rsem, device_id=dev, device_id_type=MESH)


def greet(pos, core):
    barrier = pltpu.get_barrier_semaphore()
    peers = [device(pos, 1 - core)]
    for axis in ("y", "z", "x"):
        for d in (1, 2, 3):
            peers.append(device(away(pos, axis, d), core))
    for dev in peers:
        pl.semaphore_signal(barrier, inc=1, device_id=dev, device_id_type=MESH)
    pl.semaphore_wait(barrier, len(peers))


class Ring:
    def __init__(self, pos, core, axis, buf, got, ssem, rsem):
        self.a0 = pos[axis]
        self.buf, self.got = buf, got
        up, down = device(away(pos, axis, 1), core), device(away(pos, axis, 3), core)
        far, nxt, prv = (lax.rem(self.a0 + d, 4) for d in (2, 1, 3))
        self.nxt, self.prv = nxt, prv
        route = ((far, 0, up), (far, 1, down), (nxt, 1, up), (prv, 0, down), (nxt, 0, up), (prv, 1, down))
        self.copies = [
            remote(buf.at[k, half], got.at[i], ssem.at[i], rsem.at[i], dev) for i, (k, half, dev) in enumerate(route)]

    def start(self):
        for c in self.copies[:4]:
            c.start()

    def relay(self):
        for i, k, half in ((0, self.nxt, 0), (1, self.prv, 1)):
            self.copies[i].wait_recv()
            total = self.buf[k, half].astype(f32) + self.got[i].astype(f32)
            self.buf[k, half] = total.astype(bf16)
            self.copies[4 + i].start()

    def finish(self):
        for i in (2, 3, 4, 5):
            self.copies[i].wait_recv()
        sums = []
        for half, i, j in ((0, 4, 3), (1, 2, 5)):
            sums.append(self.buf[self.a0, half].astype(f32) + self.got[i].astype(f32) + self.got[j].astype(f32))
        return sums

    def drain(self):
        for c in self.copies:
            c.wait_send()


def weight_part(p, left, left_r, right, right_r, core, g_s, out):
    own = pl.ds(pl.multiple_of(core * HALF + p * PART, PART), PART)
    theirs = pl.ds(p * PART, PART)

    @pl.loop(0, 4)
    def _(i):
        rows = pl.ds(pl.multiple_of(i * 384, 384), 384)
        g = dot_tn(left[:, rows], right[:, own]) + dot_tn(left_r[:, rows], right_r[:, theirs])
        if p == 0:
            for half in range(2):
                out[i, half] = g[half * 192:(half + 1) * 192].astype(bf16)
        else:
            g_s[i] = g

    def piece(y, z, x):
        return g_s[y, (z * 4 + x) * PIECE:(z * 4 + x + 1) * PIECE, :]

    if p > 0:
        for a in range(4):
            for b in range(4):
                rows = [piece(c, a, b) if p == 1 else piece(b, c, a) for c in range(4)]
                out[a, b // 2, (b % 2) * 96:(b % 2 + 1) * 96] = jnp.concatenate(rows, axis=0).astype(bf16)


def scatter_kernel(h, bg, bi, pg, e, fc1_out, fc2_out, in_out, out_out,
                   h_r, bg_r, bi_r, pg_r, g_s, s1, r1, s2, r2, q_s, u_s, v_s, w_s, x_s,
                   e_r, ey_s, ey_r, ez_s, ez_r, ex_s, ex_r,
                   pair_ss, pair_rs, ss1, rs1, ss2, rs2, ss3, rs3, ess, ers):
    pos, core = place()
    greet(pos, core)
    other = device(pos, 1 - core)
    theirs = pl.ds(pl.multiple_of((1 - core) * HALF, HALF), HALF)
    pair = [remote(src, dst, pair_ss.at[i], pair_rs.at[i], other) for i, (src, dst) in enumerate(
        ((h, h_r), (bg.at[:, theirs], bg_r), (bi, bi_r), (pg.at[:, theirs], pg_r), (e, e_r)))]
    for c in pair:
        c.start()
    rings1 = [[Ring(pos, core, ORDER[p][0], s1.at[m, p], r1.at[m, p], ss1.at[m, p], rs1.at[m, p])
               for p in range(3)] for m in range(2)]
    rings2 = [[Ring(pos, core, ORDER[p][1], s2.at[m, p], r2.at[m, p], ss2.at[m, p], rs2.at[m, p])
               for p in range(3)] for m in range(2)]
    side = {}

    def edge_start(axis, src, dst, base):
        side[axis] = []
        for d in (1, 2, 3):
            k = lax.rem(pos[axis] + d, 4)
            s = src.at[k] if axis == "y" else src
            c = remote(s, dst.at[d - 1], ess.at[base + d - 1], ers.at[base + d - 1], device(away(pos, axis, d), core))
            c.start()
            side[axis].append(c)

    def edge_finish(axis, mine, dst):
        for c in side[axis]:
            c.wait_recv()
        return mine + dst[0] + dst[1] + dst[2]

    def pass1(m, left, left_r, right, right_r):
        for p in range(3):
            weight_part(p, left, left_r, right, right_r, core, g_s, s1.at[m, p])
            rings1[m][p].start()

    def pass2(m):
        for p in range(3):
            for hb, v in enumerate(rings1[m][p].finish()):
                v = v.astype(bf16)
                for b in range(2):
                    for hc in range(2):
                        at = (b * 2 + hc) * 48
                        s2[m, p, 2 * hb + b, hc] = v[at:at + 48]
            rings2[m][p].start()

    def pass3(m):
        for p in range(3):
            for hc, v in enumerate(rings2[m][p].finish()):
                for c in range(2):
                    q_s[p, 2 * hc + c, m * PIECE:(m + 1) * PIECE, :] = v[c * PIECE:(c + 1) * PIECE]

    pair[0].wait_recv()
    pair[1].wait_recv()
    pass1(0, h, h_r, bg, bg_r)
    pair[4].wait_recv()
    for k in range(4):
        ey_s[k] = e[:, k * 384:(k + 1) * 384] + e_r[:, k * 384:(k + 1) * 384]
    edge_start("y", ey_s, ey_r, 0)
    for p in range(3):
        rings1[0][p].relay()
    pair[2].wait_recv()
    pair[3].wait_recv()
    pass1(1, bi, bi_r, pg, pg_r)
    ez_s[...] = edge_finish("y", ey_s[pos["y"]], ey_r)
    edge_start("z", ez_s, ez_r, 3)
    pass2(0)
    for p in range(3):
        rings1[1][p].relay()
    for p in range(3):
        rings2[0][p].relay()
    ex_s[...] = edge_finish("z", ez_s[...], ez_r)
    edge_start("x", ex_s, ex_r, 6)
    pass3(0)
    pass2(1)
    ee = edge_finish("x", ex_s[...], ex_r) * FACTOR
    q = pos["z"] * 8 + pos["x"] * 2 + core
    ee = pltpu.roll(ee, lax.rem(384 - 12 * q, 384), 1)
    in_out[...] = ee[0:C, 0:12]
    out_out[...] = ee[C:2 * C, 0:12]
    for p in range(3):
        rings2[1][p].relay()
    pass3(1)
    last = []
    for p in range(3):
        axis = ORDER[p][2]
        u_s[p] = q_s[p].astype(bf16)
        for d in (1, 2, 3):
            k = lax.rem(pos[axis] + d, 4)
            c = remote(u_s.at[p, k], v_s.at[p, d - 1], ss3.at[p, d - 1], rs3.at[p, d - 1], device(away(pos, axis, d), core))
            c.start()
            last.append(c)
    for p in range(3):
        for c in last[3 * p:3 * p + 3]:
            c.wait_recv()
        tot = q_s[p, pos[ORDER[p][2]]]
        for d in range(3):
            tot = tot + v_s[p, d].astype(f32)
        w_s[:, p * PART:(p + 1) * PART] = tot * FACTOR
    final = remote(w_s, x_s, pair_ss.at[5], pair_rs.at[5], other)
    final.start()
    mine = pl.ds(pl.multiple_of(core * HALF, HALF), HALF)
    final.wait_recv()
    for m, out in ((0, fc2_out), (1, fc1_out)):
        for src, cols in ((w_s, mine), (x_s, theirs)):
            v = src[m * PIECE:(m + 1) * PIECE, :]
            out[:, cols] = jnp.where(core == 0, v[0:12], v[12:24])
    for m in range(2):
        for p in range(3):
            rings1[m][p].drain()
            rings2[m][p].drain()
    for c in pair + last + side["y"] + side["z"] + side["x"] + [final]:
        c.wait_send()


def scatter_call(h, bg, bi, pg, e):
    v = pl.BlockSpec(memory_space=pltpu.VMEM)
    O = jax.ShapeDtypeStruct
    V = pltpu.VMEM
    D = pltpu.SemaphoreType.DMA
    return pl.pallas_call(
        scatter_kernel,
        out_shape=[O((12, W), f32), O((12, W), f32), O((C, 12), f32), O((C, 12), f32)],
        in_specs=[v] * 5,
        out_specs=[v] * 4,
        scratch_shapes=[
            V((R, W), bf16), V((R, HALF), bf16), V((R, W), bf16), V((R, HALF), bf16), V((4, 384, PART), f32),
            V((2, 3, 4, 2, 192, PART), bf16), V((2, 3, 6, 192, PART), bf16),
            V((2, 3, 4, 2, 48, PART), bf16), V((2, 3, 6, 48, PART), bf16),
            V((3, 4, 48, PART), f32), V((3, 4, 48, PART), bf16), V((3, 3, 48, PART), bf16),
            V((48, HALF), f32), V((48, HALF), f32),
            V((2 * C, W), f32), V((4, 2 * C, 384), f32), V((3, 2 * C, 384), f32),
            V((2 * C, 384), f32), V((3, 2 * C, 384), f32), V((2 * C, 384), f32), V((3, 2 * C, 384), f32),
            D((6,)), D((6,)), D((2, 3, 6)), D((2, 3, 6)), D((2, 3, 6)), D((2, 3, 6)), D((3, 3)), D((3, 3)), D((9,)), D((9,)),
        ],
        compiler_params=pltpu.CompilerParams(
            collective_id=0, has_side_effects=True, vmem_limit_bytes=56 * 1024 * 1024),
        cost_estimate=pl.CostEstimate(flops=4 * R * W * W, bytes_accessed=10_000_000, transcendentals=0),
    )(h, bg, bi, pg, e)


def body(modulation, latents, noise, times, image_rows, in_weight, fc1_weight, fc2_weight, out_weight):
    mod_grad, h, bg, bi, pg, e = local_call(
        modulation, latents, noise, times, image_rows, in_weight, fc1_weight, fc2_weight, out_weight)
    fc1_grad, fc2_grad, in_grad, out_grad = scatter_call(h, bg, bi, pg, e)
    return mod_grad, fc1_grad, fc2_grad, in_grad, out_grad


def solution(mesh):
    rows = P(("seq", "head"), None)
    cols = P(None, ("seq", "head"))
    return jax.shard_map(
        body, mesh=mesh, in_specs=(rows, rows, rows, rows, P(("seq", "head")), P(), P(), P(), P()),
        out_specs=(rows, rows, rows, cols, cols), check_vma=False)
```

```python
import jax
import jax.numpy as jnp
from jax import lax
from jax.experimental import pallas as pl
from jax.experimental.pallas import tpu as pltpu
from jax.sharding import PartitionSpec as P

f32, bf16 = jnp.float32, jnp.bfloat16
EPS = 1e-6
W, C, DRAWS, ROWS, NB = 1536, 16, 4, 128, 256
R = DRAWS * ROWS
NT = (((1,), (1,)), ((), ()))
TN = (((0,), (0,)), ((), ()))


def dot(a, b):
    return jnp.dot(a, b, preferred_element_type=f32)


def dot_nt(a, b):
    return lax.dot_general(a, b, NT, preferred_element_type=f32)


def dot_tn(a, b):
    return lax.dot_general(a, b, TN, preferred_element_type=f32)


def columns(j, base=0):
    return pl.ds(pl.multiple_of(base + j * NB, NB), NB)


def draw(k):
    return slice(k * ROWS, (k + 1) * ROWS)


def make_noisy(lat, noise, times, noisy_s):
    ang = (0.5 * jnp.pi) * times[...].astype(f32)
    cosv, sinv = jnp.cos(ang), jnp.sin(ang)
    latv = lat[...].astype(f32)
    for k in range(DRAWS):
        nz = noise[C * k:C * (k + 1), :].astype(f32)
        noisy_s[:, draw(k)] = (cosv[k:k + 1, :] * latv + sinv[k:k + 1, :] * nz).astype(bf16)


def stream(noisy_s, inw, st_s):
    @pl.loop(0, W // NB)
    def _(j):
        st_s[:, columns(j)] = dot_tn(noisy_s[...], inw[:, columns(j)])


def norm_in(mod, st_s, ni_s, ri_s, bi_s):
    @pl.loop(0, ROWS // 16)
    def _(i):
        t0 = pl.multiple_of(i * 16, 16)
        t = pl.ds(t0, 16)
        for k in range(DRAWS):
            r = pl.ds(pl.multiple_of(k * ROWS + t0, 16), 16)
            x = st_s[r, :]
            c = x - jnp.mean(x, axis=-1, keepdims=True)
            rs = lax.rsqrt(jnp.mean(c * c, axis=-1, keepdims=True) + EPS)
            n = c * rs
            ni_s[r, :] = n
            ri_s[r, :] = rs
            bi_s[r, :] = (n * (1.0 + mod[t, W:2 * W].astype(f32)) + mod[t, 0:W].astype(f32)).astype(bf16)


def fc1_fwd(bi_s, fc1, h_s, d_s):
    @pl.loop(0, W // NB)
    def _(j):
        hp = dot(bi_s[...], fc1[:, columns(j)])
        sg = jax.nn.sigmoid(hp)
        h_s[:, columns(j)] = (hp * sg).astype(bf16)
        d_s[:, columns(j)] = sg * (1.0 + hp * (1.0 - sg))


def fc2_fwd(mod, h_s, fc2, st_s, bo_s):
    @pl.loop(0, W // NB)
    def _(j):
        bo = dot(h_s[...], fc2[:, columns(j)])
        bo_s[:, columns(j)] = bo
        gate = mod[:, columns(j, 2 * W)].astype(f32)
        for k in range(DRAWS):
            st_s[draw(k), columns(j)] = st_s[draw(k), columns(j)] + gate * bo[draw(k)]


def norm_out(st_s, ro_s, fin_s):
    @pl.loop(0, R // 32)
    def _(i):
        r = pl.ds(pl.multiple_of(i * 32, 32), 32)
        x = st_s[r, :]
        c = x - jnp.mean(x, axis=-1, keepdims=True)
        rs = lax.rsqrt(jnp.mean(c * c, axis=-1, keepdims=True) + EPS)
        n = c * rs
        st_s[r, :] = n
        ro_s[r, :] = rs
        fin_s[r, :] = n.astype(bf16)


def predict(cnt, noise, fin_s, outw, pd_s, m_s):
    pred = dot_nt(outw[...], fin_s[...])
    ows = jnp.sum(outw[...].astype(f32), axis=-1, keepdims=True) * (1.0 / W)
    live = (lax.broadcasted_iota(jnp.int32, (1, ROWS), 1) < cnt[0]).astype(f32)
    for k in range(DRAWS):
        p = pred[:, draw(k)]
        pd = (2.0 * (p - noise[C * k:C * (k + 1), :].astype(f32)) * live).astype(bf16)
        pd_s[:, draw(k)] = pd
        pf = pd.astype(f32)
        m1 = jnp.sum(pf * ows, axis=0, keepdims=True)
        m2 = jnp.sum(pf * p, axis=0, keepdims=True) * (1.0 / W)
        m = jnp.concatenate([m1, m2, jnp.zeros((6, ROWS), f32)], axis=0)
        m_s[draw(k), :] = m.T


def stream_grad(mod, pd_s, outw, st_s, ro_s, m_s, bo_s, bg_s, mod_out, order, span):
    @pl.loop(*span)
    def _(i):
        j = order(i)
        fg = dot_tn(pd_s[...], outw[:, columns(j)])
        gate = mod[:, columns(j, 2 * W)].astype(f32)
        acc = None
        for k in range(DRAWS):
            r = draw(k)
            sg = ro_s[r, :] * (fg[r] - m_s[r, 0:1] - st_s[r, columns(j)] * m_s[r, 1:2])
            bg_s[r, columns(j)] = (sg * gate).astype(bf16)
            t = sg * bo_s[r, columns(j)]
            bo_s[r, columns(j)] = sg
            acc = t if acc is None else acc + t
        mod_out[:, columns(j, 2 * W)] = acc


def pre_grad(bg_s, fc2, d_s, pg_s, order, span):
    @pl.loop(*span)
    def _(i):
        j = order(i)
        ag = dot_nt(bg_s[...], fc2[columns(j), :])
        pg_s[:, columns(j)] = (ag * d_s[:, columns(j)]).astype(bf16)


def block_grad(mod, pg_s, fc1, ni_s, blk_s, a1_s, a2_s, mod_out, span):
    @pl.loop(*span)
    def _(j):
        blk = dot_nt(pg_s[...], fc1[columns(j), :])
        sp = 1.0 + mod[:, columns(j, W)].astype(f32)
        s0 = s1 = None
        for k in range(DRAWS):
            r = draw(k)
            n = ni_s[r, columns(j)]
            b = blk[r]
            bn = b * n
            g = b * sp
            blk_s[r, columns(j)] = g
            gn = g * n
            a1_s[r, :] = a1_s[r, :] + (g[:, :128] + g[:, 128:])
            a2_s[r, :] = a2_s[r, :] + (gn[:, :128] + gn[:, 128:])
            s0 = b if s0 is None else s0 + b
            s1 = bn if s1 is None else s1 + bn
        mod_out[:, columns(j)] = s0
        mod_out[:, columns(j, W)] = s1


def input_grad(ri_s, ni_s, sg_s, blk_s, a1_s, a2_s, ib_s):
    @pl.loop(0, R // 32)
    def _(i):
        r = pl.ds(pl.multiple_of(i * 32, 32), 32)
        m1 = jnp.sum(a1_s[r, :], axis=-1, keepdims=True) * (1.0 / W)
        m2 = jnp.sum(a2_s[r, :], axis=-1, keepdims=True) * (1.0 / W)
        v = sg_s[r, :] + ri_s[r, :] * (blk_s[r, :] - m1 - ni_s[r, :] * m2)
        ib_s[r, :] = v.astype(bf16)


MESH = pl.DeviceIdType.MESH
ORDER = (("y", "z", "x"), ("z", "x", "y"), ("x", "y", "z"))
HALF, PART, PIECE = W // 2, W // 6, 24
FACTOR = (ROWS * 128 // 2) ** -0.5
SEQ, HEAD = 16, 8
GROUP = W // SEQ


def place():
    s, h = lax.axis_index("seq"), lax.axis_index("head")
    return {"y": lax.div(s, 4), "z": lax.rem(s, 4), "x": lax.div(h, 2)}, lax.rem(h, 2)


def away(pos, axis, d):
    out = dict(pos)
    out[axis] = lax.rem(pos[axis] + d, 4)
    return out


def device(pos, core):
    return (pos["y"] * 4 + pos["z"], pos["x"] * 2 + core)


def remote(src, dst, ssem, rsem, dev):
    return pltpu.make_async_remote_copy(
        src_ref=src, dst_ref=dst, send_sem=ssem, recv_sem=rsem, device_id=dev, device_id_type=MESH)


def peers(pos, core):
    s, h = lax.axis_index("seq"), lax.axis_index("head")
    out = [(lax.rem(s + d, SEQ), h) for d in range(1, SEQ)]
    out += [(s, lax.rem(h + d, HEAD)) for d in range(1, HEAD)]
    out += [device(away(pos, axis, d), 1 - core) for axis in ("y", "z") for d in (1, 2, 3)]
    return out


class Ring:
    def __init__(self, pos, core, axis, buf, got, ssem, rsem):
        self.a0 = pos[axis]
        self.buf, self.got = buf, got
        up, down = device(away(pos, axis, 1), core), device(away(pos, axis, 3), core)
        far, nxt, prv = (lax.rem(self.a0 + d, 4) for d in (2, 1, 3))
        self.nxt, self.prv = nxt, prv
        route = ((far, 0, up), (far, 1, down), (nxt, 1, up), (prv, 0, down), (nxt, 0, up), (prv, 1, down))
        self.copies = [
            remote(buf.at[k, half], got.at[i], ssem.at[i], rsem.at[i], dev) for i, (k, half, dev) in enumerate(route)]

    def start(self):
        for c in self.copies[:4]:
            c.start()

    def relay(self):
        for i, k, half in ((0, self.nxt, 0), (1, self.prv, 1)):
            self.copies[i].wait_recv()
            total = self.buf[k, half].astype(f32) + self.got[i].astype(f32)
            self.buf[k, half] = total.astype(bf16)
            self.copies[4 + i].start()

    def finish(self):
        for i in (2, 3, 4, 5):
            self.copies[i].wait_recv()
        sums = []
        for half, i, j in ((0, 4, 3), (1, 2, 5)):
            sums.append(self.buf[self.a0, half].astype(f32) + self.got[i].astype(f32) + self.got[j].astype(f32))
        return sums

    def drain(self):
        for c in self.copies:
            c.wait_send()


class Direct:
    def __init__(self, pos, core, axis, buf, got, ssem, rsem):
        self.a0 = pos[axis]
        self.buf, self.got = buf, got
        self.copies = []
        for i, d in enumerate((2, 1, 3)):
            k = lax.rem(self.a0 + d, 4)
            for half in range(2):
                n = 2 * i + half
                self.copies.append(remote(buf.at[k, half], got.at[n], ssem.at[n], rsem.at[n], device(away(pos, axis, d), core)))

    def start(self):
        for c in self.copies:
            c.start()

    def relay(self):
        pass

    def finish(self):
        for c in self.copies:
            c.wait_recv()
        return [self.buf[self.a0, half].astype(f32) + self.got[half].astype(f32) + self.got[2 + half].astype(f32)
                + self.got[4 + half].astype(f32) for half in range(2)]

    def drain(self):
        for c in self.copies:
            c.wait_send()


def weight_part(p, left, left_r, right, right_r, core, g_s, out):
    own = pl.ds(pl.multiple_of(core * HALF + p * PART, PART), PART)
    theirs = pl.ds(p * PART, PART)

    @pl.loop(0, 4)
    def _(i):
        rows = pl.ds(pl.multiple_of(i * 384, 384), 384)
        g = dot_tn(left[:, rows], right[:, own]) + dot_tn(left_r[:, rows], right_r[:, theirs])
        if p == 0:
            for half in range(2):
                out[i, half] = g[half * 192:(half + 1) * 192].astype(bf16)
        else:
            g_s[i] = g

    def piece(y, z, x):
        return g_s[y, (z * 4 + x) * PIECE:(z * 4 + x + 1) * PIECE, :]

    if p > 0:
        for a in range(4):
            for b in range(4):
                rows = [piece(c, a, b) if p == 1 else piece(b, c, a) for c in range(4)]
                out[a, b // 2, (b % 2) * 96:(b % 2 + 1) * 96] = jnp.concatenate(rows, axis=0).astype(bf16)


def kernel(cnt, mod, lat, noise, times, inw, fc1_hbm, fc2_hbm, outw,
           mod_hbm, g_out, e_out,
           noisy_s, st_s, ni_s, ri_s, d_s, bo_s, ro_s, fin_s, pd_s, m_s, a1_s, a2_s,
           h, bg, bi, pg, mod_out, fc1, fc2,
           h_r, bg_r, bi_r, pg_r, g_s, s1, r1, s2, r2, q_s, u_s, l_r, e_s, ec_s, ec_r, e2_s, e2_r,
           load_sem, store_sem, pair_ss, pair_rs, ss1, rs1, ss2, rs2, ss3, rs3, ess, ers, fss, frs):
    pos, core = place()
    seq, head = lax.axis_index("seq"), lax.axis_index("head")
    barrier = pltpu.get_barrier_semaphore()
    met = peers(pos, core)
    for dev in met:
        pl.semaphore_signal(barrier, inc=1, device_id=dev, device_id_type=MESH)
    loads = [pltpu.make_async_copy(src, dst, load_sem.at[i]) for i, (src, dst) in enumerate(((fc1_hbm, fc1), (fc2_hbm, fc2)))]
    for c in loads:
        c.start()

    make_noisy(lat, noise, times, noisy_s)
    stream(noisy_s, inw, st_s)
    norm_in(mod, st_s, ni_s, ri_s, bi)
    pl.semaphore_wait(barrier, len(met))

    other = device(pos, 1 - core)
    theirs = pl.ds(pl.multiple_of((1 - core) * HALF, HALF), HALF)
    pair = [remote(src, dst, pair_ss.at[i], pair_rs.at[i], other) for i, (src, dst) in enumerate(
        ((bi, bi_r), (h, h_r), (bg.at[:, theirs], bg_r), (pg.at[:, theirs], pg_r)))]
    rings1 = [[Ring(pos, core, ORDER[p][0], s1.at[m, p], r1.at[m, p], ss1.at[m, p], rs1.at[m, p])
               for p in range(3)] for m in range(2)]
    rings2 = [[(Ring, Direct)[m](pos, core, ORDER[p][1], s2.at[m, p], r2.at[m, p], ss2.at[m, p], rs2.at[m, p])
               for p in range(3)] for m in range(2)]
    stores = [pltpu.make_async_copy(mod_out.at[:, b * W:(b + 1) * W], mod_hbm.at[:, b * W:(b + 1) * W], store_sem.at[b])
              for b in range(3)]

    def order(i):
        return lax.rem(i + 3 * (1 - core), 6)

    def pass1(m, left, left_r, right, right_r):
        for p in range(3):
            weight_part(p, left, left_r, right, right_r, core, g_s, s1.at[m, p])
            rings1[m][p].start()

    def pass2(m):
        for p in range(3):
            for hb, v in enumerate(rings1[m][p].finish()):
                v = v.astype(bf16)
                for b in range(2):
                    for hc in range(2):
                        at = (b * 2 + hc) * 48
                        s2[m, p, 2 * hb + b, hc] = v[at:at + 48]
            rings2[m][p].start()

    def pass3(m):
        for p in range(3):
            for hc, v in enumerate(rings2[m][p].finish()):
                for c in range(2):
                    q_s[p, 2 * hc + c, m * PIECE:(m + 1) * PIECE, :] = v[c * PIECE:(c + 1) * PIECE]

    def relays(rings):
        for r in rings:
            r.relay()

    pair[0].start()
    loads[0].wait()
    fc1_fwd(bi, fc1, h, d_s)
    pair[1].start()
    loads[1].wait()
    fc2_fwd(mod, h, fc2, st_s, bo_s)
    norm_out(st_s, ro_s, fin_s)
    predict(cnt, noise, fin_s, outw, pd_s, m_s)
    stream_grad(mod, pd_s, outw, st_s, ro_s, m_s, bo_s, bg, mod_out, order, (0, 3))
    pair[2].start()
    stream_grad(mod, pd_s, outw, st_s, ro_s, m_s, bo_s, bg, mod_out, order, (3, 6))
    stores[2].start()
    pair[1].wait_recv()
    pair[2].wait_recv()
    pass1(0, h, h_r, bg, bg_r)
    pre_grad(bg, fc2, d_s, pg, order, (0, 3))
    pair[3].start()
    relays(rings1[0])
    pre_grad(bg, fc2, d_s, pg, order, (3, 6))
    pair[0].wait_recv()
    pair[3].wait_recv()
    pass1(1, bi, bi_r, pg, pg_r)
    e_s[C:2 * C, 0:W] = dot(pd_s[...], fin_s[...])
    e_s[:, W:] = jnp.zeros((2 * C, 128), f32)
    a1_s[...] = jnp.zeros_like(a1_s)
    a2_s[...] = jnp.zeros_like(a2_s)
    block_grad(mod, pg, fc1, ni_s, st_s, a1_s, a2_s, mod_out, (0, 3))
    pass2(0)
    block_grad(mod, pg, fc1, ni_s, st_s, a1_s, a2_s, mod_out, (3, 6))
    stores[0].start()
    stores[1].start()
    relays(rings1[1])
    relays(rings2[0])
    input_grad(ri_s, ni_s, bo_s, st_s, a1_s, a2_s, fin_s)
    e_s[0:C, 0:W] = dot(noisy_s[...], fin_s[...])
    for k in range(SEQ):
        ec_s[k] = e_s[:, GROUP * k:GROUP * k + 128].astype(bf16)
    edge1 = [remote(ec_s.at[lax.rem(seq + d, SEQ)], ec_r.at[d - 1], ess.at[d - 1], ers.at[d - 1],
                    (lax.rem(seq + d, SEQ), head)) for d in range(1, SEQ)]
    for c in edge1:
        c.start()
    pass3(0)
    pass2(1)
    tot = ec_s[seq].astype(f32)
    for i, c in enumerate(edge1):
        c.wait_recv()
        tot = tot + ec_r[i].astype(f32)
    e2_s[...] = tot
    edge2 = [remote(e2_s, e2_r.at[d - 1], fss.at[d - 1], frs.at[d - 1], (seq, lax.rem(head + d, HEAD)))
             for d in range(1, HEAD)]
    for c in edge2:
        c.start()
    pass3(1)
    last = {}
    for p in range(3):
        axis = ORDER[p][2]
        for k in range(4):
            for c in range(2):
                v = [q_s[p, k, m * PIECE + c * 12:m * PIECE + c * 12 + 12] for m in range(2)]
                z = jnp.zeros((4, PART), f32)
                u_s[p, k, c] = jnp.concatenate([v[0], z, v[1], z], axis=0).astype(bf16)
        for rel in range(2):
            for d in range(1 - rel, 4):
                c = core if rel == 0 else 1 - core
                cp = remote(u_s.at[p, lax.rem(pos[axis] + d, 4), c], l_r.at[p, rel, d], ss3.at[p, rel, d],
                            rs3.at[p, rel, d], device(away(pos, axis, d), c))
                cp.start()
                last[p, rel, d] = cp
    for i, c in enumerate(edge2):
        c.wait_recv()
        tot = tot + e2_r[i]
    e_out[...] = pltpu.roll(tot * FACTOR, lax.rem(128 - 12 * head, 128), 1)
    mine = core * HALF
    for p in range(3):
        for rel in range(2):
            v = u_s[p, pos[ORDER[p][2]], core].astype(f32) if rel == 0 else None
            for d in range(1 - rel, 4):
                last[p, rel, d].wait_recv()
                t = l_r[p, rel, d].astype(f32)
                v = t if v is None else v + t
            v = v * FACTOR
            base = mine if rel == 0 else HALF - mine
            cols = pl.ds(pl.multiple_of(base + p * PART, PART), PART)
            g_out[:, cols] = v
    for m in range(2):
        for p in range(3):
            rings1[m][p].drain()
            rings2[m][p].drain()
    for c in pair + edge1 + edge2 + list(last.values()):
        c.wait_send()
    for c in stores:
        c.wait()


def fused_call(mod, lat, noise, times, cnt, inw, fc1, fc2, outw):
    v = pl.BlockSpec(memory_space=pltpu.VMEM)
    hbm = pl.BlockSpec(memory_space=pl.ANY)
    O = jax.ShapeDtypeStruct
    V = pltpu.VMEM
    D = pltpu.SemaphoreType.DMA
    big = V((R, W), bf16)
    half = V((R, HALF), bf16)
    return pl.pallas_call(
        kernel,
        out_shape=[O((ROWS, 3 * W), f32), O((32, W), f32), O((2 * C, 128), f32)],
        in_specs=[pl.BlockSpec(memory_space=pltpu.SMEM)] + [v] * 5 + [hbm, hbm, v],
        out_specs=[hbm, v, v],
        scratch_shapes=[
            V((C, R), bf16), V((R, W), f32), V((R, W), f32), V((R, 1), f32), V((R, W), f32), V((R, W), f32), V((R, 1), f32),
            big, V((C, R), bf16), V((R, 8), f32), V((R, 128), f32), V((R, 128), f32),
            big, big, big, big, V((ROWS, 3 * W), f32), V((W, W), bf16), V((W, W), bf16),
            big, half, big, half, V((4, 384, PART), f32),
            V((2, 3, 4, 2, 192, PART), bf16), V((2, 3, 6, 192, PART), bf16),
            V((2, 3, 4, 2, 48, PART), bf16), V((2, 3, 6, 48, PART), bf16),
            V((3, 4, 48, PART), f32), V((3, 4, 2, 32, PART), bf16), V((3, 2, 4, 32, PART), bf16),
            V((2 * C, W + 128), f32), V((SEQ, 2 * C, 128), bf16), V((SEQ - 1, 2 * C, 128), bf16),
            V((2 * C, 128), f32), V((HEAD - 1, 2 * C, 128), f32),
            D((2,)), D((3,)), D((4,)), D((4,)), D((2, 3, 6)), D((2, 3, 6)), D((2, 3, 6)), D((2, 3, 6)),
            D((3, 2, 4)), D((3, 2, 4)), D((SEQ - 1,)), D((SEQ - 1,)), D((HEAD - 1,)), D((HEAD - 1,)),
        ],
        compiler_params=pltpu.CompilerParams(
            collective_id=0, has_side_effects=True, vmem_limit_bytes=60 * 1024 * 1024),
        cost_estimate=pl.CostEstimate(flops=12 * R * W * W, bytes_accessed=20_000_000, transcendentals=R * W),
    )(cnt, mod, lat.T, noise.T, times.T, inw, fc1, fc2, outw)


def split_kernel(mod_hbm, g, e, mod_out, fc1_out, fc2_out, in_out, out_out, sem):
    c = pltpu.make_async_copy(mod_hbm, mod_out, sem)
    c.start()
    fc2_out[...] = g[0:12]
    fc1_out[...] = g[16:28]
    in_out[...] = e[0:C, 0:12]
    out_out[...] = e[C:2 * C, 0:12]
    c.wait()


def split_call(mod_grad, g, e):
    v = pl.BlockSpec(memory_space=pltpu.VMEM)
    hbm = pl.BlockSpec(memory_space=pl.ANY)
    O = jax.ShapeDtypeStruct
    return pl.pallas_call(
        split_kernel,
        out_shape=[O((ROWS, 3 * W), f32), O((12, W), f32), O((12, W), f32), O((C, 12), f32), O((C, 12), f32)],
        in_specs=[hbm, v, v],
        out_specs=[hbm, v, v, v, v],
        scratch_shapes=[pltpu.SemaphoreType.DMA],
    )(mod_grad, g, e)


def body(modulation, latents, noise, times, image_rows, in_weight, fc1_weight, fc2_weight, out_weight):
    mod_grad, g, e = fused_call(
        modulation, latents, noise, times, image_rows, in_weight, fc1_weight, fc2_weight, out_weight)
    return tuple(split_call(mod_grad, g, e))


def solution(mesh):
    rows = P(("seq", "head"), None)
    cols = P(None, ("seq", "head"))
    return jax.shard_map(
        body, mesh=mesh, in_specs=(rows, rows, rows, rows, P(("seq", "head")), P(), P(), P(), P()),
        out_specs=(rows, rows, rows, cols, cols), check_vma=False)
```

```python
import jax
import jax.numpy as jnp
from jax import lax
from jax.experimental import pallas as pl
from jax.experimental.pallas import tpu as pltpu
from jax.sharding import PartitionSpec as P

f32, bf16 = jnp.float32, jnp.bfloat16
EPS = 1e-6
W, C, DRAWS, ROWS, NB = 1536, 16, 4, 128, 256
R = DRAWS * ROWS
NT = (((1,), (1,)), ((), ()))
TN = (((0,), (0,)), ((), ()))


def dot(a, b):
    return jnp.dot(a, b, preferred_element_type=f32)


def dot_nt(a, b):
    return lax.dot_general(a, b, NT, preferred_element_type=f32)


def dot_tn(a, b):
    return lax.dot_general(a, b, TN, preferred_element_type=f32)


def columns(j, base=0):
    if isinstance(j, int):
        return slice(base + j * NB, base + (j + 1) * NB)
    return pl.ds(pl.multiple_of(base + j * NB, NB), NB)


def draw(k):
    return slice(k * ROWS, (k + 1) * ROWS)


def make_noisy(lat, noise, times, noisy_s):
    ang = (0.5 * jnp.pi) * times[...].astype(f32)
    cosv, sinv = jnp.cos(ang), jnp.sin(ang)
    latv = lat[...].astype(f32)
    for k in range(DRAWS):
        nz = noise[C * k:C * (k + 1), :].astype(f32)
        noisy_s[:, draw(k)] = (cosv[k:k + 1, :] * latv + sinv[k:k + 1, :] * nz).astype(bf16)


def stream(noisy_s, inw, st_s):
    for j in range(W // NB):
        st_s[:, columns(j)] = dot_tn(noisy_s[...], inw[:, columns(j)])


def norm_in(mod, st_s, ni_s, ri_s, bi_s):
    for t0 in range(0, ROWS, 16):
        t = slice(t0, t0 + 16)
        for k in range(DRAWS):
            r = slice(k * ROWS + t0, k * ROWS + t0 + 16)
            x = st_s[r, :]
            c = x - jnp.mean(x, axis=-1, keepdims=True)
            rs = lax.rsqrt(jnp.mean(c * c, axis=-1, keepdims=True) + EPS)
            n = c * rs
            ni_s[r, :] = n
            ri_s[r, :] = rs
            bi_s[r, :] = (n * (1.0 + mod[t, W:2 * W].astype(f32)) + mod[t, 0:W].astype(f32)).astype(bf16)


def fc1_fwd(bi_s, fc1, h_s, d_s):
    for j in range(W // NB):
        hp = dot(bi_s[0:R, :], fc1[:, columns(j)])
        sg = jax.nn.sigmoid(hp)
        h_s[0:R, columns(j)] = (hp * sg).astype(bf16)
        d_s[:, columns(j)] = sg * (1.0 + hp * (1.0 - sg))


def fc2_fwd(mod, h_s, fc2, st_s, bo_s):
    for j in range(W // NB):
        bo = dot(h_s[0:R, :], fc2[:, columns(j)])
        bo_s[:, columns(j)] = bo
        gate = mod[:, columns(j, 2 * W)].astype(f32)
        for k in range(DRAWS):
            st_s[draw(k), columns(j)] = st_s[draw(k), columns(j)] + gate * bo[draw(k)]


def norm_out(st_s, ro_s, fin_s):
    for i in range(R // 32):
        r = slice(i * 32, (i + 1) * 32)
        x = st_s[r, :]
        c = x - jnp.mean(x, axis=-1, keepdims=True)
        rs = lax.rsqrt(jnp.mean(c * c, axis=-1, keepdims=True) + EPS)
        n = c * rs
        st_s[r, :] = n
        ro_s[r, :] = rs
        fin_s[r, :] = n.astype(bf16)


def predict(cnt, noise, fin_s, outw, pd_s, m_s):
    pred = dot_nt(outw[...], fin_s[...])
    ows = jnp.sum(outw[...].astype(f32), axis=-1, keepdims=True) * (1.0 / W)
    live = (lax.broadcasted_iota(jnp.int32, (1, ROWS), 1) < cnt[0]).astype(f32)
    for k in range(DRAWS):
        p = pred[:, draw(k)]
        pd = (2.0 * (p - noise[C * k:C * (k + 1), :].astype(f32)) * live).astype(bf16)
        pd_s[:, draw(k)] = pd
        pf = pd.astype(f32)
        m1 = jnp.sum(pf * ows, axis=0, keepdims=True)
        m2 = jnp.sum(pf * p, axis=0, keepdims=True) * (1.0 / W)
        m = jnp.concatenate([m1, m2, jnp.zeros((6, ROWS), f32)], axis=0)
        m_s[draw(k), :] = m.T


def stream_grad(j, own, mod, pd_s, outw, st_s, ro_s, m_s, bo_s, bg_s, bgx_s, mod_out):
    fg = dot_tn(pd_s[...], outw[:, columns(j)])
    gate = mod[:, columns(j, 2 * W)].astype(f32)
    acc = None
    for k in range(DRAWS):
        r = draw(k)
        sg = ro_s[r, :] * (fg[r] - m_s[r, 0:1] - st_s[r, columns(j)] * m_s[r, 1:2])
        bg = (sg * gate).astype(bf16)
        bg_s[r, columns(j)] = bg
        if own is not None:
            bgx_s[r, columns(own)] = bg
        t = sg * bo_s[r, columns(j)]
        bo_s[r, columns(j)] = sg
        acc = t if acc is None else acc + t
    mod_out[:, columns(j, 2 * W)] = acc


def pre_grad(j, own, bg_s, fc2, d_s, pg_s, pgx_s):
    ag = dot_nt(bg_s[...], fc2[columns(j), :])
    pg = (ag * d_s[:, columns(j)]).astype(bf16)
    pg_s[:, columns(j)] = pg
    if own is not None:
        pgx_s[0:R, columns(own)] = pg


def block_grad(j, mod, pg_s, fc1, ni_s, blk_s, a1_s, a2_s, mod_out):
    blk = dot_nt(pg_s[...], fc1[columns(j), :])
    sp = 1.0 + mod[:, columns(j, W)].astype(f32)
    s0 = s1 = None
    for k in range(DRAWS):
        r = draw(k)
        n = ni_s[r, columns(j)]
        b = blk[r]
        bn = b * n
        g = b * sp
        blk_s[r, columns(j)] = g
        gn = g * n
        t1, t2 = g[:, :128] + g[:, 128:], gn[:, :128] + gn[:, 128:]
        a1_s[r, :] = t1 if j == 0 else a1_s[r, :] + t1
        a2_s[r, :] = t2 if j == 0 else a2_s[r, :] + t2
        s0 = b if s0 is None else s0 + b
        s1 = bn if s1 is None else s1 + bn
    mod_out[:, columns(j)] = s0
    mod_out[:, columns(j, W)] = s1


def input_grad(ri_s, ni_s, sg_s, blk_s, a1_s, a2_s, ib_s):
    for i in range(R // 32):
        r = slice(i * 32, (i + 1) * 32)
        m1 = jnp.sum(a1_s[r, :], axis=-1, keepdims=True) * (1.0 / W)
        m2 = jnp.sum(a2_s[r, :], axis=-1, keepdims=True) * (1.0 / W)
        v = sg_s[r, :] + ri_s[r, :] * (blk_s[r, :] - m1 - ni_s[r, :] * m2)
        ib_s[r, :] = v.astype(bf16)


MESH = pl.DeviceIdType.MESH
ORDER = (("y", "x", "z"), ("z", "y", "x"), ("x", "z", "y"))
HALF, PART, PIECE = W // 2, W // 6, 24
FACTOR = (ROWS * 128 // 2) ** -0.5
SEQ, HEAD, SPLIT = 16, 8, 4
GROUP = W // SEQ


def place():
    s, h = lax.axis_index("seq"), lax.axis_index("head")
    return {"y": lax.div(s, 4), "z": lax.rem(s, 4), "x": lax.div(h, 2)}, lax.rem(h, 2)


def away(pos, axis, d):
    out = dict(pos)
    out[axis] = lax.rem(pos[axis] + d, 4)
    return out


def device(pos, core):
    return (pos["y"] * 4 + pos["z"], pos["x"] * 2 + core)


def remote(src, dst, ssem, rsem, dev):
    return pltpu.make_async_remote_copy(
        src_ref=src, dst_ref=dst, send_sem=ssem, recv_sem=rsem, device_id=dev, device_id_type=MESH)


def peers(pos, core):
    s, h = lax.axis_index("seq"), lax.axis_index("head")
    out = [(lax.rem(s + d, SEQ), h) for d in range(1, SEQ)]
    out += [(s, lax.rem(h + d, HEAD)) for d in range(1, HEAD)]
    out += [device(away(pos, axis, d), 1 - core) for axis in ("y", "z") for d in (1, 2, 3)]
    return out


class Ring:
    def __init__(self, pos, core, axis, buf, got, ssem, rsem):
        self.a0 = pos[axis]
        self.buf, self.got = buf, got
        up, down = device(away(pos, axis, 1), core), device(away(pos, axis, 3), core)
        far, nxt, prv = (lax.rem(self.a0 + d, 4) for d in (2, 1, 3))
        self.nxt, self.prv = nxt, prv
        route = ((far, 0, up), (far, 1, down), (nxt, 1, up), (prv, 0, down), (nxt, 0, up), (prv, 1, down))
        self.copies = [
            remote(buf.at[k, half], got.at[i], ssem.at[i], rsem.at[i], dev) for i, (k, half, dev) in enumerate(route)]

    def start(self):
        for c in self.copies[:4]:
            c.start()

    def relay(self):
        for i, k, half in ((0, self.nxt, 0), (1, self.prv, 1)):
            self.copies[i].wait_recv()
            total = self.buf[k, half].astype(f32) + self.got[i].astype(f32)
            self.buf[k, half] = total.astype(bf16)
            self.copies[4 + i].start()

    def finish(self):
        for i in (2, 3, 4, 5):
            self.copies[i].wait_recv()
        sums = []
        for half, i, j in ((0, 4, 3), (1, 2, 5)):
            sums.append(self.buf[self.a0, half].astype(f32) + self.got[i].astype(f32) + self.got[j].astype(f32))
        return sums

    def drain(self):
        for c in self.copies:
            c.wait_send()


class Direct:
    def __init__(self, pos, core, axis, buf, got, ssem, rsem):
        self.a0 = pos[axis]
        self.buf, self.got = buf, got
        self.copies = []
        for i, d in enumerate((2, 1, 3)):
            k = lax.rem(self.a0 + d, 4)
            for half in range(2):
                n = 2 * i + half
                self.copies.append(remote(buf.at[k, half], got.at[n], ssem.at[n], rsem.at[n], device(away(pos, axis, d), core)))

    def start(self):
        for c in self.copies:
            c.start()

    def relay(self):
        pass

    def finish(self):
        for c in self.copies:
            c.wait_recv()
        return [self.buf[self.a0, half].astype(f32) + self.got[half].astype(f32) + self.got[2 + half].astype(f32)
                + self.got[4 + half].astype(f32) for half in range(2)]

    def drain(self):
        for c in self.copies:
            c.wait_send()


def weight_part(p, left, right, out):
    prev = None
    for y in range(4):
        g = dot_tn(left[:, y * 384:(y + 1) * 384], right[:, p * PART:(p + 1) * PART])
        if p == 0:
            for x in range(4):
                v = jnp.concatenate([g[(z * 4 + x) * PIECE:(z * 4 + x + 1) * PIECE] for z in range(4)], axis=0)
                out[y, x // 2, (x % 2) * 96:(x % 2 + 1) * 96] = v.astype(bf16)
        elif p == 1:
            for z in range(4):
                out[z, y // 2, (y % 2) * 96:(y % 2 + 1) * 96] = g[z * 96:(z + 1) * 96].astype(bf16)
        elif y % 2 == 1:
            for z in range(4):
                for x in range(4):
                    at = (z * 4 + x) * PIECE
                    v = jnp.concatenate([prev[at:at + PIECE], g[at:at + PIECE]], axis=0)
                    to = (z % 2) * 96 + (y // 2) * 48
                    out[x, z // 2, to:to + 48] = v.astype(bf16)
        prev = g


def kernel(cnt, mod_in, lat, noise, times, inw, fc1_hbm, fc2_hbm, outw,
           mod_hbm, g_out, e_out,
           mod, noisy_s, st_s, ni_s, ri_s, d_s, bo_s, ro_s, fin_s, pd_s, m_s, a1_s, a2_s,
           hx, bix, bg, bgx, pg, pgx, mod_out, fc1, fc2,
           s1, r1, s2, r2, q_s, u_s, l_r, e_s, ec_s, ec_r, e2_s, e2_r,
           load_sem, store_sem, pair_ss, pair_rs, ss1, rs1, ss2, rs2, ss3, rs3, ess, ers, fss, frs):
    pos, core = place()
    seq, head = lax.axis_index("seq"), lax.axis_index("head")
    barrier = pltpu.get_barrier_semaphore()
    loads = [pltpu.make_async_copy(src, dst, load_sem.at[i])
             for i, (src, dst) in enumerate(((mod_in, mod), (fc1_hbm, fc1), (fc2_hbm, fc2)))]
    for c in loads:
        c.start()
    met = peers(pos, core)
    for dev in met:
        pl.semaphore_signal(barrier, inc=1, device_id=dev, device_id_type=MESH)

    make_noisy(lat, noise, times, noisy_s)
    stream(noisy_s, inw, st_s)
    loads[0].wait()
    norm_in(mod, st_s, ni_s, ri_s, bix)
    pl.semaphore_wait(barrier, len(met))

    other = device(pos, 1 - core)
    mine, theirs = core * 3, (1 - core) * 3
    low, high = pl.ds(0, R), pl.ds(R, R)
    pair = {}

    def to_pair(name, n, src, dst):
        pair[name] = remote(src, dst, pair_ss.at[n], pair_rs.at[n], other)
        pair[name].start()

    rings1 = [[Ring(pos, core, ORDER[p][0], s1.at[m, p], r1.at[m, p], ss1.at[m, p], rs1.at[m, p])
               for p in range(3)] for m in range(2)]
    rings2 = [[(Ring, Direct)[m](pos, core, ORDER[p][1], s2.at[m, p], r2.at[m, p], ss2.at[m, p], rs2.at[m, p])
               for p in range(3)] for m in range(2)]
    stores = [pltpu.make_async_copy(mod_out.at[:, b * W:(b + 1) * W], mod_hbm.at[:, b * W:(b + 1) * W], store_sem.at[b])
              for b in range(3)]

    def pass1(m, left, right, name):
        for p in range(3):
            pair[name, p].wait_recv()
            weight_part(p, left, right, s1.at[m, p])
            rings1[m][p].start()

    def pass2(m, p):
        for hb, v in enumerate(rings1[m][p].finish()):
            v = v.astype(bf16)
            for b in range(2):
                for hc in range(2):
                    at = (b * 2 + hc) * 48
                    s2[m, p, 2 * hb + b, hc] = v[at:at + 48]
        rings2[m][p].start()

    def pass3(m, p):
        for hc, v in enumerate(rings2[m][p].finish()):
            for c in range(2):
                q_s[p, 2 * hc + c, m * PIECE:(m + 1) * PIECE, :] = v[c * PIECE:(c + 1) * PIECE]

    to_pair("bi", 0, bix.at[low], bix.at[high])
    loads[1].wait()
    fc1_fwd(bix, fc1, hx, d_s)
    to_pair("h", 1, hx.at[low], hx.at[high])
    loads[2].wait()
    fc2_fwd(mod, hx, fc2, st_s, bo_s)
    norm_out(st_s, ro_s, fin_s)
    predict(cnt, noise, fin_s, outw, pd_s, m_s)
    for i in range(6):
        j = (theirs if i < 3 else mine) + i % 3
        stream_grad(j, i - 3 if i >= 3 else None, mod, pd_s, outw, st_s, ro_s, m_s, bo_s, bg, bgx, mod_out)
        if i < 3:
            to_pair(("bg", i), 2 + i, bg.at[:, columns(j)], bgx.at[high, columns(i)])
    stores[2].start()
    pair["h"].wait_recv()
    pass1(0, hx, bgx, "bg")
    for i in range(6):
        j = (theirs if i < 3 else mine) + i % 3
        pre_grad(j, i - 3 if i >= 3 else None, bg, fc2, d_s, pg, pgx)
        if i < 3:
            to_pair(("pg", i), 5 + i, pg.at[:, columns(j)], pgx.at[high, columns(i)])
        else:
            rings1[0][i - 3].relay()
    pair["bi"].wait_recv()
    pass1(1, bix, pgx, "pg")
    e_s[C:2 * C, 0:W] = dot(pd_s[...], fin_s[...])
    e_s[:, W:] = jnp.zeros((2 * C, 128), f32)
    for j in range(6):
        block_grad(j, mod, pg, fc1, ni_s, st_s, a1_s, a2_s, mod_out)
        if j >= 3:
            pass2(0, j - 3)
    stores[0].start()
    stores[1].start()
    for p in range(3):
        rings1[1][p].relay()
    for p in range(3):
        rings2[0][p].relay()
    input_grad(ri_s, ni_s, bo_s, st_s, a1_s, a2_s, fin_s)
    e_s[0:C, 0:W] = dot(noisy_s[...], fin_s[...])
    for k in range(SEQ):
        ec_s[k] = e_s[:, GROUP * k:GROUP * k + 128].astype(bf16)
    edge1 = [remote(ec_s.at[lax.rem(seq + d, SEQ)], ec_r.at[d - 1], ess.at[d - 1], ers.at[d - 1],
                    (lax.rem(seq + d, SEQ), head)) for d in range(1, SEQ)]
    for c in edge1:
        c.start()
    for p in range(3):
        pass3(0, p)
    for p in range(3):
        pass2(1, p)
    tot = ec_s[seq].astype(f32)
    for i, c in enumerate(edge1):
        c.wait_recv()
        tot = tot + ec_r[i].astype(f32)
    e2_s[...] = tot
    edge2 = [remote(e2_s, e2_r.at[d - 1], fss.at[d - 1], frs.at[d - 1], (seq, lax.rem(head + d, HEAD)))
             for d in range(1, HEAD)]
    for c in edge2:
        c.start()
    last = {}
    for p in range(3):
        pass3(1, p)
        axis = ORDER[p][2]
        for k in range(4):
            for c in range(2):
                v = [q_s[p, k, m * PIECE + c * 12:m * PIECE + c * 12 + 12] for m in range(2)]
                z = jnp.zeros((4, PART), f32)
                u_s[p, k, c] = jnp.concatenate([v[0], z, v[1], z], axis=0).astype(bf16)
        for rel in range(2):
            for d in range(1 - rel, 4):
                c = core if rel == 0 else 1 - core
                cp = remote(u_s.at[p, lax.rem(pos[axis] + d, 4), c], l_r.at[p, rel, d], ss3.at[p, rel, d],
                            rs3.at[p, rel, d], device(away(pos, axis, d), c))
                cp.start()
                last[p, rel, d] = cp
    for i, c in enumerate(edge2):
        c.wait_recv()
        tot = tot + e2_r[i]
    e_out[...] = pltpu.roll(tot * FACTOR, lax.rem(128 - 12 * head, 128), 1)
    for p in range(3):
        for rel in range(2):
            v = u_s[p, pos[ORDER[p][2]], core].astype(f32) if rel == 0 else None
            for d in range(1 - rel, 4):
                last[p, rel, d].wait_recv()
                t = l_r[p, rel, d].astype(f32)
                v = t if v is None else v + t
            g_out[:, columns((mine if rel == 0 else theirs) + p)] = v * FACTOR
    for m in range(2):
        for p in range(3):
            rings1[m][p].drain()
            rings2[m][p].drain()
    for c in list(pair.values()) + edge1 + edge2 + list(last.values()):
        c.wait_send()
    for c in stores:
        c.wait()


def fused_call(mod, lat, noise, times, cnt, inw, fc1, fc2, outw):
    v = pl.BlockSpec(memory_space=pltpu.VMEM)
    hbm = pl.BlockSpec(memory_space=pl.ANY)
    O = jax.ShapeDtypeStruct
    V = pltpu.VMEM
    D = pltpu.SemaphoreType.DMA
    big = V((R, W), bf16)
    two = V((2 * R, W), bf16)
    half = V((2 * R, HALF), bf16)
    return pl.pallas_call(
        kernel,
        out_shape=[O((ROWS, 3 * W), f32), O((32, W), f32), O((2 * C, 128), f32)],
        in_specs=[pl.BlockSpec(memory_space=pltpu.SMEM), hbm, v, v, v, v, hbm, hbm, v],
        out_specs=[hbm, v, v],
        scratch_shapes=[
            V((ROWS, 3 * W), bf16), V((C, R), bf16), V((R, W), f32), V((R, W), f32), V((R, 1), f32), V((R, W), f32),
            V((R, W), f32), V((R, 1), f32), big, V((C, R), bf16), V((R, 8), f32), V((R, 128), f32), V((R, 128), f32),
            two, two, big, half, big, half, V((ROWS, 3 * W), f32), V((W, W), bf16), V((W, W), bf16),
            V((2, 3, 4, 2, 192, PART), bf16), V((2, 3, 6, 192, PART), bf16),
            V((2, 3, 4, 2, 48, PART), bf16), V((2, 3, 6, 48, PART), bf16),
            V((3, 4, 48, PART), f32), V((3, 4, 2, 32, PART), bf16), V((3, 2, 4, 32, PART), bf16),
            V((2 * C, W + 128), f32), V((SEQ, 2 * C, 128), bf16), V((SEQ - 1, 2 * C, 128), bf16),
            V((2 * C, 128), f32), V((HEAD - 1, 2 * C, 128), f32),
            D((3,)), D((3,)), D((8,)), D((8,)), D((2, 3, 6)), D((2, 3, 6)), D((2, 3, 6)), D((2, 3, 6)),
            D((3, 2, 4)), D((3, 2, 4)), D((SEQ - 1,)), D((SEQ - 1,)), D((HEAD - 1,)), D((HEAD - 1,)),
        ],
        compiler_params=pltpu.CompilerParams(
            collective_id=0, has_side_effects=True, vmem_limit_bytes=60 * 1024 * 1024),
        cost_estimate=pl.CostEstimate(flops=12 * R * W * W, bytes_accessed=20_000_000, transcendentals=R * W),
    )(cnt, mod, lat.T, noise.T, times.T, inw, fc1, fc2, outw)


def split_kernel(mod_hbm, g, e, mod_out, fc1_out, fc2_out, in_out, out_out, buf, in_sem, out_sem):
    n = ROWS // SPLIT
    parts = [pl.ds(i * n, n) for i in range(SPLIT)]
    into = [pltpu.make_async_copy(mod_hbm.at[r], buf.at[r], in_sem.at[i]) for i, r in enumerate(parts)]
    out = [pltpu.make_async_copy(buf.at[r], mod_out.at[r], out_sem.at[i]) for i, r in enumerate(parts)]
    for c in into:
        c.start()
    fc2_out[...] = g[0:12]
    fc1_out[...] = g[16:28]
    in_out[...] = e[0:C, 0:12]
    out_out[...] = e[C:2 * C, 0:12]
    for a, b in zip(into, out):
        a.wait()
        b.start()
    for c in out:
        c.wait()


def split_call(mod_grad, g, e):
    v = pl.BlockSpec(memory_space=pltpu.VMEM)
    hbm = pl.BlockSpec(memory_space=pl.ANY)
    O = jax.ShapeDtypeStruct
    return pl.pallas_call(
        split_kernel,
        out_shape=[O((ROWS, 3 * W), f32), O((12, W), f32), O((12, W), f32), O((C, 12), f32), O((C, 12), f32)],
        in_specs=[hbm, v, v],
        out_specs=[hbm, v, v, v, v],
        scratch_shapes=[pltpu.VMEM((ROWS, 3 * W), f32), pltpu.SemaphoreType.DMA((SPLIT,)), pltpu.SemaphoreType.DMA((SPLIT,))],
        compiler_params=pltpu.CompilerParams(vmem_limit_bytes=60 * 1024 * 1024),
    )(mod_grad, g, e)


def body(modulation, latents, noise, times, image_rows, in_weight, fc1_weight, fc2_weight, out_weight):
    mod_grad, g, e = fused_call(
        modulation, latents, noise, times, image_rows, in_weight, fc1_weight, fc2_weight, out_weight)
    return tuple(split_call(mod_grad, g, e))


def solution(mesh):
    rows = P(("seq", "head"), None)
    cols = P(None, ("seq", "head"))
    return jax.shard_map(
        body, mesh=mesh, in_specs=(rows, rows, rows, rows, P(("seq", "head")), P(), P(), P(), P()),
        out_specs=(rows, rows, rows, cols, cols), check_vma=False)
```

```python
import jax
import jax.numpy as jnp
from jax import lax
from jax.experimental import pallas as pl
from jax.experimental.pallas import tpu as pltpu
from jax.sharding import PartitionSpec as P

f32, bf16 = jnp.float32, jnp.bfloat16
EPS = 1e-6
W, C, DRAWS, ROWS, NB = 1536, 16, 4, 128, 256
R = DRAWS * ROWS
NT = (((1,), (1,)), ((), ()))
TN = (((0,), (0,)), ((), ()))


def dot(a, b):
    return jnp.dot(a, b, preferred_element_type=f32)


def dot_nt(a, b):
    return lax.dot_general(a, b, NT, preferred_element_type=f32)


def dot_tn(a, b):
    return lax.dot_general(a, b, TN, preferred_element_type=f32)


def columns(j, base=0):
    if isinstance(j, int):
        return slice(base + j * NB, base + (j + 1) * NB)
    return pl.ds(pl.multiple_of(base + j * NB, NB), NB)


def draw(k):
    return slice(k * ROWS, (k + 1) * ROWS)


def make_noisy(lat, noise, times, noisy_s):
    ang = (0.5 * jnp.pi) * times[...].astype(f32)
    cosv, sinv = jnp.cos(ang), jnp.sin(ang)
    latv = lat[...].astype(f32)
    for k in range(DRAWS):
        nz = noise[C * k:C * (k + 1), :].astype(f32)
        noisy_s[:, draw(k)] = (cosv[k:k + 1, :] * latv + sinv[k:k + 1, :] * nz).astype(bf16)


def stream(noisy_s, inw, st_s):
    for j in range(W // NB):
        st_s[:, columns(j)] = dot_tn(noisy_s[...], inw[:, columns(j)])


def norm_in(mod, st_s, ni_s, ri_s, bi_s):
    for t0 in range(0, ROWS, 16):
        t = slice(t0, t0 + 16)
        for k in range(DRAWS):
            r = slice(k * ROWS + t0, k * ROWS + t0 + 16)
            x = st_s[r, :]
            c = x - jnp.mean(x, axis=-1, keepdims=True)
            rs = lax.rsqrt(jnp.mean(c * c, axis=-1, keepdims=True) + EPS)
            n = c * rs
            ni_s[r, :] = n
            ri_s[r, :] = rs
            bi_s[r, :] = (n * (1.0 + mod[t, W:2 * W].astype(f32)) + mod[t, 0:W].astype(f32)).astype(bf16)


def fc1_fwd(bi_s, fc1, h_s, d_s):
    for j in range(W // NB):
        hp = dot(bi_s[0:R, :], fc1[:, columns(j)])
        sg = jax.nn.sigmoid(hp)
        h_s[0:R, columns(j)] = (hp * sg).astype(bf16)
        d_s[:, columns(j)] = sg * (1.0 + hp * (1.0 - sg))


def fc2_fwd(mod, h_s, fc2, st_s, bo_s):
    for j in range(W // NB):
        bo = dot(h_s[0:R, :], fc2[:, columns(j)])
        bo_s[:, columns(j)] = bo
        gate = mod[:, columns(j, 2 * W)].astype(f32)
        for k in range(DRAWS):
            st_s[draw(k), columns(j)] = st_s[draw(k), columns(j)] + gate * bo[draw(k)]


def norm_out(k, st_s, ro_s, fin_s):
    for i in range(ROWS // 32):
        r = slice(k * ROWS + i * 32, k * ROWS + (i + 1) * 32)
        x = st_s[r, :]
        c = x - jnp.mean(x, axis=-1, keepdims=True)
        rs = lax.rsqrt(jnp.mean(c * c, axis=-1, keepdims=True) + EPS)
        n = c * rs
        st_s[r, :] = n
        ro_s[r, :] = rs
        fin_s[r, :] = n.astype(bf16)


def predict(k, cnt, noise, fin_s, outw, pd_s, m_s):
    p = dot_nt(outw[...], fin_s[draw(k), :])
    ows = jnp.sum(outw[...].astype(f32), axis=-1, keepdims=True) * (1.0 / W)
    live = (lax.broadcasted_iota(jnp.int32, (1, ROWS), 1) < cnt[0]).astype(f32)
    pd = (2.0 * (p - noise[C * k:C * (k + 1), :].astype(f32)) * live).astype(bf16)
    pd_s[:, draw(k)] = pd
    pf = pd.astype(f32)
    m1 = jnp.sum(pf * ows, axis=0, keepdims=True)
    m2 = jnp.sum(pf * p, axis=0, keepdims=True) * (1.0 / W)
    m = jnp.concatenate([m1, m2, jnp.zeros((6, ROWS), f32)], axis=0)
    m_s[draw(k), :] = m.T


def stream_grad(j, own, mod, pd_s, outw, st_s, ro_s, m_s, sg_s, bg_s, bgx_s):
    fg = dot_tn(pd_s[...], outw[:, columns(j)])
    gate = mod[:, columns(j, 2 * W)].astype(f32)
    for k in range(DRAWS):
        r = draw(k)
        sg = ro_s[r, :] * (fg[r] - m_s[r, 0:1] - st_s[r, columns(j)] * m_s[r, 1:2])
        bg = (sg * gate).astype(bf16)
        sg_s[r, columns(j)] = sg
        bg_s[r, columns(j)] = bg
        if own is not None:
            bgx_s[r, columns(own)] = bg


def pre_grad(j, own, bg_s, fc2, d_s, pg_s, pgx_s):
    ag = dot_nt(bg_s[...], fc2[columns(j), :])
    pg = (ag * d_s[:, columns(j)]).astype(bf16)
    pg_s[:, columns(j)] = pg
    if own is not None:
        pgx_s[0:R, columns(own)] = pg


def block_grad(j, mod, pg_s, fc1, ni_s, sg_s, bo_s, blk_s, a1_s, a2_s, mod_out):
    blk = dot_nt(pg_s[...], fc1[columns(j), :])
    sp = 1.0 + mod[:, columns(j, W)].astype(f32)
    s0 = s1 = s2 = None
    for k in range(DRAWS):
        r = draw(k)
        n = ni_s[r, columns(j)]
        b = blk[r]
        bn = b * n
        g = b * sp
        blk_s[r, columns(j)] = g
        gn = g * n
        t1, t2 = g[:, :128] + g[:, 128:], gn[:, :128] + gn[:, 128:]
        a1_s[r, :] = t1 if j == 0 else a1_s[r, :] + t1
        a2_s[r, :] = t2 if j == 0 else a2_s[r, :] + t2
        s0 = b if s0 is None else s0 + b
        s1 = bn if s1 is None else s1 + bn
        t = sg_s[r, columns(j)] * bo_s[r, columns(j)]
        s2 = t if s2 is None else s2 + t
    mod_out[:, columns(j)] = s0
    mod_out[:, columns(j, W)] = s1
    mod_out[:, columns(j, 2 * W)] = s2


def input_grad(ri_s, ni_s, sg_s, blk_s, a1_s, a2_s, ib_s):
    for i in range(R // 32):
        r = slice(i * 32, (i + 1) * 32)
        m1 = jnp.sum(a1_s[r, :], axis=-1, keepdims=True) * (1.0 / W)
        m2 = jnp.sum(a2_s[r, :], axis=-1, keepdims=True) * (1.0 / W)
        v = sg_s[r, :] + ri_s[r, :] * (blk_s[r, :] - m1 - ni_s[r, :] * m2)
        ib_s[r, :] = v.astype(bf16)


MESH = pl.DeviceIdType.MESH
ORDER = (("y", "x", "z"), ("z", "y", "x"), ("x", "z", "y"))
HALF, PART, PIECE = W // 2, W // 6, 24
FACTOR = (ROWS * 128 // 2) ** -0.5
SEQ, HEAD, SPLIT = 16, 8, 4
GROUP = W // SEQ


def place():
    s, h = lax.axis_index("seq"), lax.axis_index("head")
    return {"y": lax.div(s, 4), "z": lax.rem(s, 4), "x": lax.div(h, 2)}, lax.rem(h, 2)


def away(pos, axis, d):
    out = dict(pos)
    out[axis] = lax.rem(pos[axis] + d, 4)
    return out


def device(pos, core):
    return (pos["y"] * 4 + pos["z"], pos["x"] * 2 + core)


def remote(src, dst, ssem, rsem, dev):
    return pltpu.make_async_remote_copy(
        src_ref=src, dst_ref=dst, send_sem=ssem, recv_sem=rsem, device_id=dev, device_id_type=MESH)


def peers(pos, core):
    s, h = lax.axis_index("seq"), lax.axis_index("head")
    out = [(lax.rem(s + d, SEQ), h) for d in range(1, SEQ)]
    out += [(s, lax.rem(h + d, HEAD)) for d in range(1, HEAD)]
    out += [device(away(pos, axis, d), 1 - core) for axis in ("y", "z") for d in (1, 2, 3)]
    return out


class Ring:
    def __init__(self, pos, core, axis, buf, got, ssem, rsem):
        self.a0 = pos[axis]
        self.buf, self.got = buf, got
        up, down = device(away(pos, axis, 1), core), device(away(pos, axis, 3), core)
        far, nxt, prv = (lax.rem(self.a0 + d, 4) for d in (2, 1, 3))
        self.nxt, self.prv = nxt, prv
        route = ((far, 0, up), (far, 1, down), (nxt, 1, up), (prv, 0, down), (nxt, 0, up), (prv, 1, down))
        self.copies = [
            remote(buf.at[k, half], got.at[i], ssem.at[i], rsem.at[i], dev) for i, (k, half, dev) in enumerate(route)]

    def start(self):
        self.start_far()
        self.start_near()

    def start_far(self):
        for c in self.copies[:2]:
            c.start()

    def start_near(self):
        for c in self.copies[2:4]:
            c.start()

    def relay(self):
        for i, k, half in ((0, self.nxt, 0), (1, self.prv, 1)):
            self.copies[i].wait_recv()
            total = self.buf[k, half].astype(f32) + self.got[i].astype(f32)
            self.buf[k, half] = total.astype(bf16)
            self.copies[4 + i].start()

    def finish(self):
        for i in (2, 3, 4, 5):
            self.copies[i].wait_recv()
        sums = []
        for half, i, j in ((0, 4, 3), (1, 2, 5)):
            sums.append(self.buf[self.a0, half].astype(f32) + self.got[i].astype(f32) + self.got[j].astype(f32))
        return sums

    def drain(self):
        for c in self.copies:
            c.wait_send()


class Direct:
    def __init__(self, pos, core, axis, buf, got, ssem, rsem):
        self.a0 = pos[axis]
        self.buf, self.got = buf, got
        self.copies = []
        for i, d in enumerate((2, 1, 3)):
            k = lax.rem(self.a0 + d, 4)
            for half in range(2):
                n = 2 * i + half
                self.copies.append(remote(buf.at[k, half], got.at[n], ssem.at[n], rsem.at[n], device(away(pos, axis, d), core)))

    def start(self):
        for c in self.copies:
            c.start()

    def relay(self):
        pass

    def finish(self):
        for c in self.copies:
            c.wait_recv()
        return [self.buf[self.a0, half].astype(f32) + self.got[half].astype(f32) + self.got[2 + half].astype(f32)
                + self.got[4 + half].astype(f32) for half in range(2)]

    def drain(self):
        for c in self.copies:
            c.wait_send()


def weight_own(left, right, acc):
    for y in range(2):
        acc[y] = dot_tn(left[0:R, y * 384:(y + 1) * 384], right[0:R, :])


def weight_parts(left, right, acc, out):
    prev = None
    for y in range(4):
        rows = slice(y * 384, (y + 1) * 384)
        if y < 2:
            g = acc[y] + dot_tn(left[R:2 * R, rows], right[R:2 * R, :])
        else:
            g = dot_tn(left[:, rows], right[...])
        g0, g1, g2 = (g[:, p * PART:(p + 1) * PART] for p in range(3))
        for x in range(4):
            v = jnp.concatenate([g0[(z * 4 + x) * PIECE:(z * 4 + x + 1) * PIECE] for z in range(4)], axis=0)
            out[0, y, x // 2, (x % 2) * 96:(x % 2 + 1) * 96] = v.astype(bf16)
        for z in range(4):
            out[1, z, y // 2, (y % 2) * 96:(y % 2 + 1) * 96] = g1[z * 96:(z + 1) * 96].astype(bf16)
        if y % 2 == 1:
            for z in range(4):
                for x in range(4):
                    at = (z * 4 + x) * PIECE
                    v = jnp.concatenate([prev[at:at + PIECE], g2[at:at + PIECE]], axis=0)
                    to = (z % 2) * 96 + (y // 2) * 48
                    out[2, x, z // 2, to:to + 48] = v.astype(bf16)
        prev = g2


def kernel(cnt, mod_in, lat, noise, times, inw, fc1_hbm, fc2_hbm, outw,
           mod_hbm, g_out, e_out,
           mod, noisy_s, st_s, ni_s, ri_s, d_s, bo_s, sg_s, ro_s, fin_s, pd_s, m_s, a1_s, a2_s,
           hx, bix, bg, bgx, pg, pgx, mod_out, fc1, fc2,
           acc, s1, r1, s2, r2, u_s, l_r, e_s, ec_s, ec_r, e2_s, e2_r, g_s, ee_s,
           load_sem, store_sem, pair_ss, pair_rs, ss1, rs1, ss2, rs2, ss3, rs3, ess, ers, fss, frs, out_sem):
    pos, core = place()
    seq, head = lax.axis_index("seq"), lax.axis_index("head")
    barrier = pltpu.get_barrier_semaphore()
    def load(n, src, dst):
        return [pltpu.make_async_copy(src.at[pl.ds(i * 384, 384)], dst.at[pl.ds(i * 384, 384)], load_sem.at[n, i])
                for i in range(4)]

    def wait(copies):
        for c in copies:
            c.wait()

    mod_load = pltpu.make_async_copy(mod_in, mod, load_sem.at[2, 0])
    mod_load.start()
    fc1_load, fc2_load = load(0, fc1_hbm, fc1), load(1, fc2_hbm, fc2)
    for c in fc1_load:
        c.start()
    met = peers(pos, core)
    for dev in met:
        pl.semaphore_signal(barrier, inc=1, device_id=dev, device_id_type=MESH)

    make_noisy(lat, noise, times, noisy_s)
    stream(noisy_s, inw, st_s)
    mod_load.wait()
    norm_in(mod, st_s, ni_s, ri_s, bix)
    pl.semaphore_wait(barrier, len(met))

    other = device(pos, 1 - core)
    mine, theirs = core * 3, (1 - core) * 3
    half_at = pl.ds(pl.multiple_of((1 - core) * HALF, HALF), HALF)
    low, high = pl.ds(0, R), pl.ds(R, R)
    pair = {}

    def to_pair(name, n, src, dst):
        pair[name] = remote(src, dst, pair_ss.at[n], pair_rs.at[n], other)
        pair[name].start()

    rings1 = [[Ring(pos, core, ORDER[p][0], s1.at[m, p], r1.at[m, p], ss1.at[m, p], rs1.at[m, p])
               for p in range(3)] for m in range(2)]
    rings2 = [[Direct(pos, core, ORDER[p][1], s2.at[m, p], r2.at[m, p], ss2.at[m, p], rs2.at[m, p])
               for p in range(3)] for m in range(2)]
    stores = [pltpu.make_async_copy(mod_out.at[:, b * W:(b + 1) * W], mod_hbm.at[:, b * W:(b + 1) * W], store_sem.at[b])
              for b in range(3)]

    def each(m, name):
        for p in range(3):
            getattr(rings1[m][p], name)()

    def pass2(m, p):
        for hb, v in enumerate(rings1[m][p].finish()):
            v = v.astype(bf16)
            for b in range(2):
                for hc in range(2):
                    at = (b * 2 + hc) * 48
                    s2[m, p, 2 * hb + b, hc] = v[at:at + 48]
        rings2[m][p].start()

    def pass3(m, p):
        z = jnp.zeros((4, PART), f32)
        for hc, v in enumerate(rings2[m][p].finish()):
            for k in range(2):
                for c in range(2):
                    at = k * PIECE + c * 12
                    u_s[m, p, 2 * hc + k, c] = jnp.concatenate([v[at:at + 12], z], axis=0).astype(bf16)

    def finish_part(m, p):
        pass3(m, p)
        axis = ORDER[p][2]
        for rel in range(2):
            for d in range(1 - rel, 4):
                c = core if rel == 0 else 1 - core
                cp = remote(u_s.at[m, p, lax.rem(pos[axis] + d, 4), c], l_r.at[m, p, rel, d], ss3.at[m, p, rel, d],
                            rs3.at[m, p, rel, d], device(away(pos, axis, d), c))
                cp.start()
                last[m, p, rel, d] = cp

    out_copies = [pltpu.make_async_copy(g_s.at[pl.ds(16 * m, 16)], g_out.at[pl.ds(16 * m, 16)], out_sem.at[m]) for m in range(2)]
    out_copies.append(pltpu.make_async_copy(ee_s, e_out, out_sem.at[2]))

    def take(m):
        for p in range(3):
            for rel in range(2):
                v = u_s[m, p, pos[ORDER[p][2]], core].astype(f32) if rel == 0 else None
                for d in range(1 - rel, 4):
                    last[m, p, rel, d].wait_recv()
                    t = l_r[m, p, rel, d].astype(f32)
                    v = t if v is None else v + t
                g_s[m * 16:(m + 1) * 16, columns((mine if rel == 0 else theirs) + p)] = v * FACTOR
        out_copies[m].start()

    to_pair("bi", 0, bix.at[low], bix.at[high])
    wait(fc1_load)
    for c in fc2_load:
        c.start()
    fc1_fwd(bix, fc1, hx, d_s)
    to_pair("h", 1, hx.at[low], hx.at[high])
    wait(fc2_load)
    fc2_fwd(mod, hx, fc2, st_s, bo_s)
    for k in range(DRAWS):
        norm_out(k, st_s, ro_s, fin_s)
        predict(k, cnt, noise, fin_s, outw, pd_s, m_s)
    for i in range(3):
        stream_grad(theirs + i, None, mod, pd_s, outw, st_s, ro_s, m_s, sg_s, bg, bgx)
    to_pair("bg", 2, bg.at[:, half_at], bgx.at[high])
    for i in range(3):
        stream_grad(mine + i, i, mod, pd_s, outw, st_s, ro_s, m_s, sg_s, bg, bgx)
    weight_own(hx, bgx, acc)
    pair["h"].wait_recv()
    pair["bg"].wait_recv()
    weight_parts(hx, bgx, acc, s1.at[0])
    each(0, "start_far")
    each(0, "start_near")
    for i in range(3):
        pre_grad(theirs + i, None, bg, fc2, d_s, pg, pgx)
    to_pair("pg", 3, pg.at[:, half_at], pgx.at[high])
    for i in range(3):
        pre_grad(mine + i, i, bg, fc2, d_s, pg, pgx)
    weight_own(bix, pgx, acc)
    each(0, "relay")
    pair["bi"].wait_recv()
    pair["pg"].wait_recv()
    weight_parts(bix, pgx, acc, s1.at[1])
    each(1, "start_far")
    each(1, "start_near")
    e_s[C:2 * C, 0:W] = dot(pd_s[...], fin_s[...])
    e_s[:, W:] = jnp.zeros((2 * C, 128), f32)
    for j in range(6):
        block_grad(j, mod, pg, fc1, ni_s, sg_s, bo_s, st_s, a1_s, a2_s, mod_out)
    for c in stores:
        c.start()
    for p in range(3):
        pass2(0, p)
    input_grad(ri_s, ni_s, sg_s, st_s, a1_s, a2_s, fin_s)
    e_s[0:C, 0:W] = dot(noisy_s[...], fin_s[...])
    for k in range(SEQ):
        ec_s[k] = e_s[:, GROUP * k:GROUP * k + 128].astype(bf16)
    each(1, "relay")
    edge1 = [remote(ec_s.at[lax.rem(seq + d, SEQ)], ec_r.at[d - 1], ess.at[d - 1], ers.at[d - 1],
                    (lax.rem(seq + d, SEQ), head)) for d in range(1, SEQ)]
    for c in edge1:
        c.start()
    for p in range(3):
        pass2(1, p)
    last = {}
    for p in range(3):
        finish_part(0, p)
    tot = ec_s[seq].astype(f32)
    for i, c in enumerate(edge1):
        c.wait_recv()
        tot = tot + ec_r[i].astype(f32)
    e2_s[...] = tot
    edge2 = [remote(e2_s, e2_r.at[d - 1], fss.at[d - 1], frs.at[d - 1], (seq, lax.rem(head + d, HEAD)))
             for d in range(1, HEAD)]
    for c in edge2:
        c.start()
    for p in range(3):
        finish_part(1, p)
    take(0)
    for i, c in enumerate(edge2):
        c.wait_recv()
        tot = tot + e2_r[i]
    ee_s[...] = pltpu.roll(tot * FACTOR, lax.rem(128 - 12 * head, 128), 1)
    out_copies[2].start()
    take(1)
    for m in range(2):
        for p in range(3):
            rings1[m][p].drain()
            rings2[m][p].drain()
    for c in list(pair.values()) + edge1 + edge2 + list(last.values()):
        c.wait_send()
    for c in stores + out_copies:
        c.wait()


def fused_call(mod, lat, noise, times, cnt, inw, fc1, fc2, outw):
    v = pl.BlockSpec(memory_space=pltpu.VMEM)
    hbm = pl.BlockSpec(memory_space=pl.ANY)
    O = jax.ShapeDtypeStruct
    V = pltpu.VMEM
    D = pltpu.SemaphoreType.DMA
    big = V((R, W), bf16)
    two = V((2 * R, W), bf16)
    half = V((2 * R, HALF), bf16)
    return pl.pallas_call(
        kernel,
        out_shape=[O((ROWS, 3 * W), f32), O((32, W), f32), O((2 * C, 128), f32)],
        in_specs=[pl.BlockSpec(memory_space=pltpu.SMEM), hbm, v, v, v, v, hbm, hbm, v],
        out_specs=[hbm, hbm, hbm],
        scratch_shapes=[
            V((ROWS, 3 * W), bf16), V((C, R), bf16), V((R, W), f32), V((R, W), f32), V((R, 1), f32), V((R, W), f32),
            V((R, W), f32), V((R, W), f32), V((R, 1), f32), big, V((C, R), bf16), V((R, 8), f32), V((R, 128), f32), V((R, 128), f32),
            two, two, big, half, big, half, V((ROWS, 3 * W), f32), V((W, W), bf16), V((W, W), bf16),
            V((2, 384, HALF), f32), V((2, 3, 4, 2, 192, PART), bf16), V((2, 3, 6, 192, PART), bf16),
            V((2, 3, 4, 2, 48, PART), bf16), V((2, 3, 6, 48, PART), bf16),
            V((2, 3, 4, 2, 16, PART), bf16), V((2, 3, 2, 4, 16, PART), bf16),
            V((2 * C, W + 128), f32), V((SEQ, 2 * C, 128), bf16), V((SEQ - 1, 2 * C, 128), bf16),
            V((2 * C, 128), f32), V((HEAD - 1, 2 * C, 128), f32), V((32, W), f32), V((2 * C, 128), f32),
            D((3, 4)), D((3,)), D((4,)), D((4,)), D((2, 3, 6)), D((2, 3, 6)), D((2, 3, 6)), D((2, 3, 6)),
            D((2, 3, 2, 4)), D((2, 3, 2, 4)), D((SEQ - 1,)), D((SEQ - 1,)), D((HEAD - 1,)), D((HEAD - 1,)), D((3,)),
        ],
        compiler_params=pltpu.CompilerParams(
            collective_id=0, has_side_effects=True, vmem_limit_bytes=62 * 1024 * 1024),
        cost_estimate=pl.CostEstimate(flops=12 * R * W * W, bytes_accessed=20_000_000, transcendentals=R * W),
    )(cnt, mod, lat.T, noise.T, times.T, inw, fc1, fc2, outw)


def split_kernel(mod_hbm, g_hbm, e_hbm, mod_out, fc1_out, fc2_out, in_out, out_out,
                 buf, g, e, fc1_s, fc2_s, in_s, out_s, in_sem, out_sem):
    n = ROWS // SPLIT
    parts = [pl.ds(i * n, n) for i in range(SPLIT)]
    into = [pltpu.make_async_copy(src, dst, in_sem.at[SPLIT + i]) for i, (src, dst) in enumerate(((g_hbm, g), (e_hbm, e)))]
    into += [pltpu.make_async_copy(mod_hbm.at[r], buf.at[r], in_sem.at[i]) for i, r in enumerate(parts)]
    small = ((fc1_s, fc1_out), (fc2_s, fc2_out), (in_s, in_out), (out_s, out_out))
    out = [pltpu.make_async_copy(src, dst, out_sem.at[SPLIT + i]) for i, (src, dst) in enumerate(small)]
    out += [pltpu.make_async_copy(buf.at[r], mod_out.at[r], out_sem.at[i]) for i, r in enumerate(parts)]
    for c in into:
        c.start()
    into[0].wait()
    into[1].wait()
    fc2_s[...] = g[0:12]
    fc1_s[...] = g[16:28]
    in_s[...] = e[0:C, 0:12]
    out_s[...] = e[C:2 * C, 0:12]
    for c in out[:4]:
        c.start()
    for a, b in zip(into[2:], out[4:]):
        a.wait()
        b.start()
    for c in out:
        c.wait()


def split_call(mod_grad, g, e):
    hbm = pl.BlockSpec(memory_space=pl.ANY)
    O = jax.ShapeDtypeStruct
    V = pltpu.VMEM
    return pl.pallas_call(
        split_kernel,
        out_shape=[O((ROWS, 3 * W), f32), O((12, W), f32), O((12, W), f32), O((C, 12), f32), O((C, 12), f32)],
        in_specs=[hbm] * 3,
        out_specs=[hbm] * 5,
        scratch_shapes=[V((ROWS, 3 * W), f32), V((32, W), f32), V((2 * C, 128), f32), V((12, W), f32), V((12, W), f32),
                        V((C, 12), f32), V((C, 12), f32),
                        pltpu.SemaphoreType.DMA((SPLIT + 2,)), pltpu.SemaphoreType.DMA((SPLIT + 4,))],
        compiler_params=pltpu.CompilerParams(vmem_limit_bytes=60 * 1024 * 1024),
    )(mod_grad, g, e)


def body(modulation, latents, noise, times, image_rows, in_weight, fc1_weight, fc2_weight, out_weight):
    mod_grad, g, e = fused_call(
        modulation, latents, noise, times, image_rows, in_weight, fc1_weight, fc2_weight, out_weight)
    return tuple(split_call(mod_grad, g, e))


def solution(mesh):
    rows = P(("seq", "head"), None)
    cols = P(None, ("seq", "head"))
    return jax.shard_map(
        body, mesh=mesh, in_specs=(rows, rows, rows, rows, P(("seq", "head")), P(), P(), P(), P()),
        out_specs=(rows, rows, rows, cols, cols), check_vma=False)
```

```python
import jax
import jax.numpy as jnp
from jax import lax
from jax.experimental import pallas as pl
from jax.experimental.pallas import tpu as pltpu
from jax.sharding import PartitionSpec as P

f32, bf16 = jnp.float32, jnp.bfloat16
EPS = 1e-6
W, C, DRAWS, ROWS, NB = 1536, 16, 4, 128, 256
R = DRAWS * ROWS
NT = (((1,), (1,)), ((), ()))
TN = (((0,), (0,)), ((), ()))


def dot(a, b):
    return jnp.dot(a, b, preferred_element_type=f32)


def dot_nt(a, b):
    return lax.dot_general(a, b, NT, preferred_element_type=f32)


def dot_tn(a, b):
    return lax.dot_general(a, b, TN, preferred_element_type=f32)


def columns(j, base=0):
    if isinstance(j, int):
        return slice(base + j * NB, base + (j + 1) * NB)
    return pl.ds(pl.multiple_of(base + j * NB, NB), NB)


def draw(k):
    return slice(k * ROWS, (k + 1) * ROWS)


def make_noisy(lat, noise, times, noisy_s):
    ang = (0.5 * jnp.pi) * times[...].astype(f32)
    cosv, sinv = jnp.cos(ang), jnp.sin(ang)
    latv = lat[...].astype(f32)
    for k in range(DRAWS):
        nz = noise[C * k:C * (k + 1), :].astype(f32)
        noisy_s[:, draw(k)] = (cosv[k:k + 1, :] * latv + sinv[k:k + 1, :] * nz).astype(bf16)


def stream(noisy_s, inw, st_s):
    for j in range(W // NB):
        st_s[:, columns(j)] = dot_tn(noisy_s[...], inw[:, columns(j)])


def norm_in(mod, st_s, ni_s, ri_s, bi_s):
    for t0 in range(0, ROWS, 16):
        t = slice(t0, t0 + 16)
        for k in range(DRAWS):
            r = slice(k * ROWS + t0, k * ROWS + t0 + 16)
            x = st_s[r, :]
            c = x - jnp.mean(x, axis=-1, keepdims=True)
            rs = lax.rsqrt(jnp.mean(c * c, axis=-1, keepdims=True) + EPS)
            n = c * rs
            ni_s[r, :] = n
            ri_s[r, :] = rs
            bi_s[r, :] = (n * (1.0 + mod[t, W:2 * W].astype(f32)) + mod[t, 0:W].astype(f32)).astype(bf16)


def fc1_fwd(bi_s, fc1, h_s, d_s):
    for j in range(W // NB):
        hp = dot(bi_s[0:R, :], fc1[:, columns(j)])
        sg = jax.nn.sigmoid(hp)
        h_s[0:R, columns(j)] = (hp * sg).astype(bf16)
        d_s[:, columns(j)] = sg * (1.0 + hp * (1.0 - sg))


def fc2_fwd(mod, h_s, fc2, st_s, bo_s):
    for j in range(W // NB):
        bo = dot(h_s[0:R, :], fc2[:, columns(j)])
        bo_s[:, columns(j)] = bo
        gate = mod[:, columns(j, 2 * W)].astype(f32)
        for k in range(DRAWS):
            st_s[draw(k), columns(j)] = st_s[draw(k), columns(j)] + gate * bo[draw(k)]


def norm_out(k, st_s, ro_s, fin_s):
    for i in range(ROWS // 32):
        r = slice(k * ROWS + i * 32, k * ROWS + (i + 1) * 32)
        x = st_s[r, :]
        c = x - jnp.mean(x, axis=-1, keepdims=True)
        rs = lax.rsqrt(jnp.mean(c * c, axis=-1, keepdims=True) + EPS)
        n = c * rs
        st_s[r, :] = n
        ro_s[r, :] = rs
        fin_s[r, :] = n.astype(bf16)


def predict(k, cnt, noise, fin_s, outw, pd_s, m_s):
    p = dot_nt(outw[...], fin_s[draw(k), :])
    ows = jnp.sum(outw[...].astype(f32), axis=-1, keepdims=True) * (1.0 / W)
    live = (lax.broadcasted_iota(jnp.int32, (1, ROWS), 1) < cnt[0]).astype(f32)
    pd = (2.0 * (p - noise[C * k:C * (k + 1), :].astype(f32)) * live).astype(bf16)
    pd_s[:, draw(k)] = pd
    pf = pd.astype(f32)
    m1 = jnp.sum(pf * ows, axis=0, keepdims=True)
    m2 = jnp.sum(pf * p, axis=0, keepdims=True) * (1.0 / W)
    m = jnp.concatenate([m1, m2, jnp.zeros((6, ROWS), f32)], axis=0)
    m_s[draw(k), :] = m.T


def stream_grad(j, own, mod, pd_s, outw, st_s, ro_s, m_s, sg_s, bg_s, bgx_s):
    fg = dot_tn(pd_s[...], outw[:, columns(j)])
    gate = mod[:, columns(j, 2 * W)].astype(f32)
    for k in range(DRAWS):
        r = draw(k)
        sg = ro_s[r, :] * (fg[r] - m_s[r, 0:1] - st_s[r, columns(j)] * m_s[r, 1:2])
        bg = (sg * gate).astype(bf16)
        sg_s[r, columns(j)] = sg
        bg_s[r, columns(j)] = bg
        if own is not None:
            bgx_s[r, columns(own)] = bg


def pre_grad(j, own, bg_s, fc2, d_s, pg_s, pgx_s):
    ag = dot_nt(bg_s[...], fc2[columns(j), :])
    pg = (ag * d_s[:, columns(j)]).astype(bf16)
    pg_s[:, columns(j)] = pg
    if own is not None:
        pgx_s[0:R, columns(own)] = pg


def block_grad(j, mod, pg_s, fc1, ni_s, sg_s, bo_s, blk_s, a1_s, a2_s, mod_out):
    blk = dot_nt(pg_s[...], fc1[columns(j), :])
    sp = 1.0 + mod[:, columns(j, W)].astype(f32)
    s0 = s1 = s2 = None
    for k in range(DRAWS):
        r = draw(k)
        n = ni_s[r, columns(j)]
        b = blk[r]
        bn = b * n
        g = b * sp
        blk_s[r, columns(j)] = g
        gn = g * n
        t1, t2 = g[:, :128] + g[:, 128:], gn[:, :128] + gn[:, 128:]
        a1_s[r, :] = t1 if j == 0 else a1_s[r, :] + t1
        a2_s[r, :] = t2 if j == 0 else a2_s[r, :] + t2
        s0 = b if s0 is None else s0 + b
        s1 = bn if s1 is None else s1 + bn
        t = sg_s[r, columns(j)] * bo_s[r, columns(j)]
        s2 = t if s2 is None else s2 + t
    mod_out[:, columns(j)] = s0
    mod_out[:, columns(j, W)] = s1
    mod_out[:, columns(j, 2 * W)] = s2


def input_grad(ri_s, ni_s, sg_s, blk_s, a1_s, a2_s, ib_s):
    for i in range(R // 32):
        r = slice(i * 32, (i + 1) * 32)
        m1 = jnp.sum(a1_s[r, :], axis=-1, keepdims=True) * (1.0 / W)
        m2 = jnp.sum(a2_s[r, :], axis=-1, keepdims=True) * (1.0 / W)
        v = sg_s[r, :] + ri_s[r, :] * (blk_s[r, :] - m1 - ni_s[r, :] * m2)
        ib_s[r, :] = v.astype(bf16)


MESH = pl.DeviceIdType.MESH
ORDER = (("y", "x", "z"), ("z", "y", "x"), ("x", "z", "y"))
HALF, PART, PIECE = W // 2, W // 6, 24
FACTOR = (ROWS * 128 // 2) ** -0.5
SEQ, HEAD, SPLIT = 16, 8, 4
GROUP = W // SEQ


def place():
    s, h = lax.axis_index("seq"), lax.axis_index("head")
    return {"y": lax.div(s, 4), "z": lax.rem(s, 4), "x": lax.div(h, 2)}, lax.rem(h, 2)


def away(pos, axis, d):
    out = dict(pos)
    out[axis] = lax.rem(pos[axis] + d, 4)
    return out


def device(pos, core):
    return (pos["y"] * 4 + pos["z"], pos["x"] * 2 + core)


def remote(src, dst, ssem, rsem, dev):
    return pltpu.make_async_remote_copy(
        src_ref=src, dst_ref=dst, send_sem=ssem, recv_sem=rsem, device_id=dev, device_id_type=MESH)


def peers(pos, core):
    s, h = lax.axis_index("seq"), lax.axis_index("head")
    out = [(lax.rem(s + d, SEQ), h) for d in range(1, SEQ)]
    out += [(s, lax.rem(h + d, HEAD)) for d in range(1, HEAD)]
    out += [device(away(pos, axis, d), 1 - core) for axis in ("y", "z") for d in (1, 2, 3)]
    return out


class Ring:
    def __init__(self, pos, core, axis, buf, got, ssem, rsem):
        self.a0 = pos[axis]
        self.buf, self.got = buf, got
        up, down = device(away(pos, axis, 1), core), device(away(pos, axis, 3), core)
        far, nxt, prv = (lax.rem(self.a0 + d, 4) for d in (2, 1, 3))
        self.nxt, self.prv = nxt, prv
        route = ((far, 0, up), (far, 1, down), (nxt, 1, up), (prv, 0, down), (nxt, 0, up), (prv, 1, down))
        self.copies = [
            remote(buf.at[k, half], got.at[i], ssem.at[i], rsem.at[i], dev) for i, (k, half, dev) in enumerate(route)]

    def start(self):
        self.start_far()
        self.start_near()

    def start_far(self):
        for c in self.copies[:2]:
            c.start()

    def start_near(self):
        for c in self.copies[2:4]:
            c.start()

    def relay(self):
        for i, k, half in ((0, self.nxt, 0), (1, self.prv, 1)):
            self.copies[i].wait_recv()
            total = self.buf[k, half].astype(f32) + self.got[i].astype(f32)
            self.buf[k, half] = total.astype(bf16)
            self.copies[4 + i].start()

    def finish(self):
        for i in (2, 3, 4, 5):
            self.copies[i].wait_recv()
        sums = []
        for half, i, j in ((0, 4, 3), (1, 2, 5)):
            sums.append(self.buf[self.a0, half].astype(f32) + self.got[i].astype(f32) + self.got[j].astype(f32))
        return sums

    def drain(self):
        for c in self.copies:
            c.wait_send()


class Direct:
    def __init__(self, pos, core, axis, buf, got, ssem, rsem):
        self.a0 = pos[axis]
        self.buf, self.got = buf, got
        self.copies = []
        for i, d in enumerate((2, 1, 3)):
            k = lax.rem(self.a0 + d, 4)
            for half in range(2):
                n = 2 * i + half
                self.copies.append(remote(buf.at[k, half], got.at[n], ssem.at[n], rsem.at[n], device(away(pos, axis, d), core)))

    def start(self):
        for c in self.copies:
            c.start()

    def relay(self):
        pass

    def finish(self):
        for c in self.copies:
            c.wait_recv()
        return [self.buf[self.a0, half].astype(f32) + self.got[half].astype(f32) + self.got[2 + half].astype(f32)
                + self.got[4 + half].astype(f32) for half in range(2)]

    def drain(self):
        for c in self.copies:
            c.wait_send()


def weight_own(left, right, acc):
    for y in range(2):
        acc[y] = dot_tn(left[0:R, y * 384:(y + 1) * 384], right[0:R, :])


def weight_parts(left, right, acc, out):
    prev = None
    for y in range(4):
        rows = slice(y * 384, (y + 1) * 384)
        if y < 2:
            g = acc[y] + dot_tn(left[R:2 * R, rows], right[R:2 * R, :])
        else:
            g = dot_tn(left[:, rows], right[...])
        g0, g1, g2 = (g[:, p * PART:(p + 1) * PART] for p in range(3))
        for x in range(4):
            v = jnp.concatenate([g0[(z * 4 + x) * PIECE:(z * 4 + x + 1) * PIECE] for z in range(4)], axis=0)
            out[0, y, x // 2, (x % 2) * 96:(x % 2 + 1) * 96] = v.astype(bf16)
        for z in range(4):
            out[1, z, y // 2, (y % 2) * 96:(y % 2 + 1) * 96] = g1[z * 96:(z + 1) * 96].astype(bf16)
        if y % 2 == 1:
            for z in range(4):
                for x in range(4):
                    at = (z * 4 + x) * PIECE
                    v = jnp.concatenate([prev[at:at + PIECE], g2[at:at + PIECE]], axis=0)
                    to = (z % 2) * 96 + (y // 2) * 48
                    out[2, x, z // 2, to:to + 48] = v.astype(bf16)
        prev = g2


def kernel(cnt, mod_in, lat_hbm, noise_hbm, times_hbm, inw_hbm, fc1_hbm, fc2_hbm, outw_hbm,
           mod_hbm, g_out, e_out,
           mod, lat, noise, times, inw, outw, noisy_s, st_s, ni_s, ri_s, d_s, bo_s, sg_s, ro_s, fin_s, pd_s, m_s, a1_s, a2_s,
           hx, bix, bg, bgx, pg, pgx, mod_out, fc1, fc2,
           acc, s1, r1, s2, r2, u_s, l_r, e_s, ec_s, ec_r, e2_s, e2_r, g_s, ee_s,
           load_sem, store_sem, pair_ss, pair_rs, ss1, rs1, ss2, rs2, ss3, rs3, ess, ers, fss, frs, out_sem):
    pos, core = place()
    seq, head = lax.axis_index("seq"), lax.axis_index("head")
    barrier = pltpu.get_barrier_semaphore()
    def load(n, src, dst):
        return [pltpu.make_async_copy(src.at[pl.ds(i * 384, 384)], dst.at[pl.ds(i * 384, 384)], load_sem.at[n, i])
                for i in range(4)]

    def wait(copies):
        for c in copies:
            c.wait()

    small = [pltpu.make_async_copy(src, dst, load_sem.at[2, i + 1]) for i, (src, dst) in enumerate(
        ((lat_hbm, lat), (noise_hbm, noise), (inw_hbm, inw), (outw_hbm, outw), (times_hbm, times)))]
    mod_load = pltpu.make_async_copy(mod_in, mod, load_sem.at[2, 0])
    fc1_load, fc2_load = load(0, fc1_hbm, fc1), load(1, fc2_hbm, fc2)
    for c in small + [mod_load] + fc1_load:
        c.start()
    met = peers(pos, core)
    for dev in met:
        pl.semaphore_signal(barrier, inc=1, device_id=dev, device_id_type=MESH)

    wait(small)
    make_noisy(lat, noise, times, noisy_s)
    stream(noisy_s, inw, st_s)
    mod_load.wait()
    norm_in(mod, st_s, ni_s, ri_s, bix)
    pl.semaphore_wait(barrier, len(met))

    other = device(pos, 1 - core)
    mine, theirs = core * 3, (1 - core) * 3
    half_at = pl.ds(pl.multiple_of((1 - core) * HALF, HALF), HALF)
    low, high = pl.ds(0, R), pl.ds(R, R)
    pair = {}

    def to_pair(name, n, src, dst):
        pair[name] = remote(src, dst, pair_ss.at[n], pair_rs.at[n], other)
        pair[name].start()

    rings1 = [[Ring(pos, core, ORDER[p][0], s1.at[m, p], r1.at[m, p], ss1.at[m, p], rs1.at[m, p])
               for p in range(3)] for m in range(2)]
    rings2 = [[Direct(pos, core, ORDER[p][1], s2.at[m, p], r2.at[m, p], ss2.at[m, p], rs2.at[m, p])
               for p in range(3)] for m in range(2)]
    stores = [pltpu.make_async_copy(mod_out.at[:, b * W:(b + 1) * W], mod_hbm.at[:, b * W:(b + 1) * W], store_sem.at[b])
              for b in range(3)]

    def each(m, name):
        for p in range(3):
            getattr(rings1[m][p], name)()

    def pass2(m, p):
        for hb, v in enumerate(rings1[m][p].finish()):
            v = v.astype(bf16)
            for b in range(2):
                for hc in range(2):
                    at = (b * 2 + hc) * 48
                    s2[m, p, 2 * hb + b, hc] = v[at:at + 48]
        rings2[m][p].start()

    def pass3(m, p):
        z = jnp.zeros((4, PART), f32)
        for hc, v in enumerate(rings2[m][p].finish()):
            for k in range(2):
                for c in range(2):
                    at = k * PIECE + c * 12
                    u_s[m, p, 2 * hc + k, c] = jnp.concatenate([v[at:at + 12], z], axis=0).astype(bf16)

    def finish_part(m, p):
        pass3(m, p)
        axis = ORDER[p][2]
        for rel in range(2):
            for d in (2, 1, 3, 0)[:3 + rel]:
                c = core if rel == 0 else 1 - core
                cp = remote(u_s.at[m, p, lax.rem(pos[axis] + d, 4), c], l_r.at[m, p, rel, d], ss3.at[m, p, rel, d],
                            rs3.at[m, p, rel, d], device(away(pos, axis, d), c))
                cp.start()
                last[m, p, rel, d] = cp

    out_copies = [pltpu.make_async_copy(g_s.at[pl.ds(16 * m, 16)], g_out.at[pl.ds(16 * m, 16)], out_sem.at[m]) for m in range(2)]
    out_copies.append(pltpu.make_async_copy(ee_s, e_out, out_sem.at[2]))

    def take(m):
        for p in range(3):
            for rel in range(2):
                v = u_s[m, p, pos[ORDER[p][2]], core].astype(f32) if rel == 0 else None
                for d in range(1 - rel, 4):
                    last[m, p, rel, d].wait_recv()
                    t = l_r[m, p, rel, d].astype(f32)
                    v = t if v is None else v + t
                g_s[m * 16:(m + 1) * 16, columns((mine if rel == 0 else theirs) + p)] = v * FACTOR
        out_copies[m].start()

    to_pair("bi", 0, bix.at[low], bix.at[high])
    wait(fc1_load)
    for c in fc2_load:
        c.start()
    fc1_fwd(bix, fc1, hx, d_s)
    to_pair("h", 1, hx.at[low], hx.at[high])
    wait(fc2_load)
    fc2_fwd(mod, hx, fc2, st_s, bo_s)
    for k in range(DRAWS):
        norm_out(k, st_s, ro_s, fin_s)
        predict(k, cnt, noise, fin_s, outw, pd_s, m_s)
    for i in range(3):
        stream_grad(theirs + i, None, mod, pd_s, outw, st_s, ro_s, m_s, sg_s, bg, bgx)
    to_pair("bg", 2, bg.at[:, half_at], bgx.at[high])
    for i in range(3):
        stream_grad(mine + i, i, mod, pd_s, outw, st_s, ro_s, m_s, sg_s, bg, bgx)
    weight_own(hx, bgx, acc)
    pair["h"].wait_recv()
    pair["bg"].wait_recv()
    weight_parts(hx, bgx, acc, s1.at[0])
    each(0, "start_far")
    each(0, "start_near")
    for i in range(3):
        pre_grad(theirs + i, None, bg, fc2, d_s, pg, pgx)
    to_pair("pg", 3, pg.at[:, half_at], pgx.at[high])
    for i in range(3):
        pre_grad(mine + i, i, bg, fc2, d_s, pg, pgx)
    weight_own(bix, pgx, acc)
    each(0, "relay")
    pair["bi"].wait_recv()
    pair["pg"].wait_recv()
    weight_parts(bix, pgx, acc, s1.at[1])
    each(1, "start_far")
    each(1, "start_near")
    e_s[C:2 * C, 0:W] = dot(pd_s[...], fin_s[...])
    e_s[:, W:] = jnp.zeros((2 * C, 128), f32)
    for j in range(6):
        block_grad(j, mod, pg, fc1, ni_s, sg_s, bo_s, st_s, a1_s, a2_s, mod_out)
    for c in stores:
        c.start()
    for p in range(3):
        pass2(0, p)
    input_grad(ri_s, ni_s, sg_s, st_s, a1_s, a2_s, fin_s)
    e_s[0:C, 0:W] = dot(noisy_s[...], fin_s[...])
    for k in range(SEQ):
        ec_s[k] = e_s[:, GROUP * k:GROUP * k + 128].astype(bf16)
    each(1, "relay")
    edge1 = [remote(ec_s.at[lax.rem(seq + d, SEQ)], ec_r.at[d - 1], ess.at[d - 1], ers.at[d - 1],
                    (lax.rem(seq + d, SEQ), head)) for d in range(1, SEQ)]
    for c in edge1:
        c.start()
    for p in range(3):
        pass2(1, p)
    last = {}
    for p in range(3):
        finish_part(0, p)
    tot = ec_s[seq].astype(f32)
    for i, c in enumerate(edge1):
        c.wait_recv()
        tot = tot + ec_r[i].astype(f32)
    e2_s[...] = tot
    edge2 = [remote(e2_s, e2_r.at[d - 1], fss.at[d - 1], frs.at[d - 1], (seq, lax.rem(head + d, HEAD)))
             for d in range(1, HEAD)]
    for c in edge2:
        c.start()
    for p in range(3):
        finish_part(1, p)
    take(0)
    for i, c in enumerate(edge2):
        c.wait_recv()
        tot = tot + e2_r[i]
    ee_s[...] = pltpu.roll(tot * FACTOR, lax.rem(128 - 12 * head, 128), 1)
    out_copies[2].start()
    take(1)
    for m in range(2):
        for p in range(3):
            rings1[m][p].drain()
            rings2[m][p].drain()
    for c in list(pair.values()) + edge1 + edge2 + list(last.values()):
        c.wait_send()
    for c in stores + out_copies:
        c.wait()


def fused_call(mod, lat, noise, times, cnt, inw, fc1, fc2, outw):
    v = pl.BlockSpec(memory_space=pltpu.VMEM)
    hbm = pl.BlockSpec(memory_space=pl.ANY)
    O = jax.ShapeDtypeStruct
    V = pltpu.VMEM
    D = pltpu.SemaphoreType.DMA
    big = V((R, W), bf16)
    two = V((2 * R, W), bf16)
    half = V((2 * R, HALF), bf16)
    return pl.pallas_call(
        kernel,
        out_shape=[O((ROWS, 3 * W), f32), O((32, W), f32), O((2 * C, 128), f32)],
        in_specs=[pl.BlockSpec(memory_space=pltpu.SMEM), hbm, hbm, hbm, hbm, hbm, hbm, hbm, hbm],
        out_specs=[hbm, hbm, hbm],
        scratch_shapes=[
            V((ROWS, 3 * W), bf16), V((C, ROWS), bf16), V((DRAWS * C, ROWS), bf16), V((DRAWS, ROWS), bf16), V((C, W), bf16), V((C, W), bf16), V((C, R), bf16), V((R, W), f32), V((R, W), f32), V((R, 1), f32), V((R, W), f32),
            V((R, W), f32), V((R, W), f32), V((R, 1), f32), big, V((C, R), bf16), V((R, 8), f32), V((R, 128), f32), V((R, 128), f32),
            two, two, big, half, big, half, V((ROWS, 3 * W), f32), V((W, W), bf16), V((W, W), bf16),
            V((2, 384, HALF), f32), V((2, 3, 4, 2, 192, PART), bf16), V((2, 3, 6, 192, PART), bf16),
            V((2, 3, 4, 2, 48, PART), bf16), V((2, 3, 6, 48, PART), bf16),
            V((2, 3, 4, 2, 16, PART), bf16), V((2, 3, 2, 4, 16, PART), bf16),
            V((2 * C, W + 128), f32), V((SEQ, 2 * C, 128), bf16), V((SEQ - 1, 2 * C, 128), bf16),
            V((2 * C, 128), f32), V((HEAD - 1, 2 * C, 128), f32), V((32, W), f32), V((2 * C, 128), f32),
            D((3, 6)), D((3,)), D((4,)), D((4,)), D((2, 3, 6)), D((2, 3, 6)), D((2, 3, 6)), D((2, 3, 6)),
            D((2, 3, 2, 4)), D((2, 3, 2, 4)), D((SEQ - 1,)), D((SEQ - 1,)), D((HEAD - 1,)), D((HEAD - 1,)), D((3,)),
        ],
        compiler_params=pltpu.CompilerParams(
            collective_id=0, has_side_effects=True, vmem_limit_bytes=62 * 1024 * 1024),
        cost_estimate=pl.CostEstimate(flops=12 * R * W * W, bytes_accessed=20_000_000, transcendentals=R * W),
    )(cnt, mod, lat.T, noise.T, times.T, inw, fc1, fc2, outw)


def split_kernel(mod_hbm, g_hbm, e_hbm, mod_out, fc1_out, fc2_out, in_out, out_out,
                 buf, g, e, fc1_s, fc2_s, in_s, out_s, in_sem, out_sem):
    n = ROWS // SPLIT
    parts = [pl.ds(i * n, n) for i in range(SPLIT)]
    into = [pltpu.make_async_copy(src, dst, in_sem.at[SPLIT + i]) for i, (src, dst) in enumerate(((g_hbm, g), (e_hbm, e)))]
    into += [pltpu.make_async_copy(mod_hbm.at[r], buf.at[r], in_sem.at[i]) for i, r in enumerate(parts)]
    small = ((fc1_s, fc1_out), (fc2_s, fc2_out), (in_s, in_out), (out_s, out_out))
    out = [pltpu.make_async_copy(src, dst, out_sem.at[SPLIT + i]) for i, (src, dst) in enumerate(small)]
    out += [pltpu.make_async_copy(buf.at[r], mod_out.at[r], out_sem.at[i]) for i, r in enumerate(parts)]
    for c in into:
        c.start()
    into[0].wait()
    into[1].wait()
    fc2_s[...] = g[0:12]
    fc1_s[...] = g[16:28]
    in_s[...] = e[0:C, 0:12]
    out_s[...] = e[C:2 * C, 0:12]
    for c in out[:4]:
        c.start()
    for a, b in zip(into[2:], out[4:]):
        a.wait()
        b.start()
    for c in out:
        c.wait()


def split_call(mod_grad, g, e):
    hbm = pl.BlockSpec(memory_space=pl.ANY)
    O = jax.ShapeDtypeStruct
    V = pltpu.VMEM
    return pl.pallas_call(
        split_kernel,
        out_shape=[O((ROWS, 3 * W), f32), O((12, W), f32), O((12, W), f32), O((C, 12), f32), O((C, 12), f32)],
        in_specs=[hbm] * 3,
        out_specs=[hbm] * 5,
        scratch_shapes=[V((ROWS, 3 * W), f32), V((32, W), f32), V((2 * C, 128), f32), V((12, W), f32), V((12, W), f32),
                        V((C, 12), f32), V((C, 12), f32),
                        pltpu.SemaphoreType.DMA((SPLIT + 2,)), pltpu.SemaphoreType.DMA((SPLIT + 4,))],
        compiler_params=pltpu.CompilerParams(vmem_limit_bytes=60 * 1024 * 1024),
    )(mod_grad, g, e)


def body(modulation, latents, noise, times, image_rows, in_weight, fc1_weight, fc2_weight, out_weight):
    mod_grad, g, e = fused_call(
        modulation, latents, noise, times, image_rows, in_weight, fc1_weight, fc2_weight, out_weight)
    return tuple(split_call(mod_grad, g, e))


def solution(mesh):
    rows = P(("seq", "head"), None)
    cols = P(None, ("seq", "head"))
    return jax.shard_map(
        body, mesh=mesh, in_specs=(rows, rows, rows, rows, P(("seq", "head")), P(), P(), P(), P()),
        out_specs=(rows, rows, rows, cols, cols), check_vma=False)
```

```python
import jax
import jax.numpy as jnp
from jax import lax
from jax.experimental import pallas as pl
from jax.experimental.pallas import tpu as pltpu
from jax.sharding import PartitionSpec as P

f32, bf16 = jnp.float32, jnp.bfloat16
EPS = 1e-6
W, C, DRAWS, ROWS, NB = 1536, 16, 4, 128, 256
R = DRAWS * ROWS
NT = (((1,), (1,)), ((), ()))
TN = (((0,), (0,)), ((), ()))


def dot(a, b):
    return jnp.dot(a, b, preferred_element_type=f32)


def dot_nt(a, b):
    return lax.dot_general(a, b, NT, preferred_element_type=f32)


def dot_tn(a, b):
    return lax.dot_general(a, b, TN, preferred_element_type=f32)


def columns(j, base=0):
    if isinstance(j, int):
        return slice(base + j * NB, base + (j + 1) * NB)
    return pl.ds(pl.multiple_of(base + j * NB, NB), NB)


def draw(k):
    return slice(k * ROWS, (k + 1) * ROWS)


def make_noisy(lat, noise, times, noisy_s):
    ang = (0.5 * jnp.pi) * times[...].astype(f32)
    cosv, sinv = jnp.cos(ang), jnp.sin(ang)
    latv = lat[...].astype(f32)
    for k in range(DRAWS):
        nz = noise[C * k:C * (k + 1), :].astype(f32)
        noisy_s[:, draw(k)] = (cosv[k:k + 1, :] * latv + sinv[k:k + 1, :] * nz).astype(bf16)


def stream(noisy_s, inw, st_s):
    for j in range(W // NB):
        st_s[:, columns(j)] = dot_tn(noisy_s[...], inw[:, columns(j)])


def norm_in(mod, st_s, ni_s, ri_s, bi_s):
    for t0 in range(0, ROWS, 16):
        t = slice(t0, t0 + 16)
        for k in range(DRAWS):
            r = slice(k * ROWS + t0, k * ROWS + t0 + 16)
            x = st_s[r, :]
            c = x - jnp.mean(x, axis=-1, keepdims=True)
            rs = lax.rsqrt(jnp.mean(c * c, axis=-1, keepdims=True) + EPS)
            n = c * rs
            ni_s[r, :] = n
            ri_s[r, :] = rs
            bi_s[r, :] = (n * (1.0 + mod[t, W:2 * W].astype(f32)) + mod[t, 0:W].astype(f32)).astype(bf16)


def fc1_fwd(bi_s, fc1, h_s, d_s):
    for j in range(W // NB):
        hp = dot(bi_s[0:R, :], fc1[:, columns(j)])
        sg = jax.nn.sigmoid(hp)
        h_s[0:R, columns(j)] = (hp * sg).astype(bf16)
        d_s[:, columns(j)] = sg * (1.0 + hp * (1.0 - sg))


def fc2_fwd(mod, h_s, fc2, st_s, bo_s):
    for j in range(W // NB):
        bo = dot(h_s[0:R, :], fc2[:, columns(j)])
        bo_s[:, columns(j)] = bo
        gate = mod[:, columns(j, 2 * W)].astype(f32)
        for k in range(DRAWS):
            st_s[draw(k), columns(j)] = st_s[draw(k), columns(j)] + gate * bo[draw(k)]


def norm_out(k, st_s, ro_s, fin_s):
    for i in range(ROWS // 32):
        r = slice(k * ROWS + i * 32, k * ROWS + (i + 1) * 32)
        x = st_s[r, :]
        c = x - jnp.mean(x, axis=-1, keepdims=True)
        rs = lax.rsqrt(jnp.mean(c * c, axis=-1, keepdims=True) + EPS)
        n = c * rs
        st_s[r, :] = n
        ro_s[r, :] = rs
        fin_s[r, :] = n.astype(bf16)


def predict(k, cnt, noise, fin_s, outw, pd_s, m_s):
    p = dot_nt(outw[...], fin_s[draw(k), :])
    ows = jnp.sum(outw[...].astype(f32), axis=-1, keepdims=True) * (1.0 / W)
    live = (lax.broadcasted_iota(jnp.int32, (1, ROWS), 1) < cnt[0]).astype(f32)
    pd = (2.0 * (p - noise[C * k:C * (k + 1), :].astype(f32)) * live).astype(bf16)
    pd_s[:, draw(k)] = pd
    pf = pd.astype(f32)
    m1 = jnp.sum(pf * ows, axis=0, keepdims=True)
    m2 = jnp.sum(pf * p, axis=0, keepdims=True) * (1.0 / W)
    m = jnp.concatenate([m1, m2, jnp.zeros((6, ROWS), f32)], axis=0)
    m_s[draw(k), :] = m.T


def stream_grad(j, own, mod, pd_s, outw, st_s, ro_s, m_s, sg_s, bg_s, bgx_s):
    fg = dot_tn(pd_s[...], outw[:, columns(j)])
    gate = mod[:, columns(j, 2 * W)].astype(f32)
    for k in range(DRAWS):
        r = draw(k)
        sg = ro_s[r, :] * (fg[r] - m_s[r, 0:1] - st_s[r, columns(j)] * m_s[r, 1:2])
        bg = (sg * gate).astype(bf16)
        sg_s[r, columns(j)] = sg
        bg_s[r, columns(j)] = bg
        if own is not None:
            bgx_s[r, columns(own)] = bg


def pre_grad(j, own, bg_s, fc2, d_s, pg_s, pgx_s):
    ag = dot_nt(bg_s[...], fc2[columns(j), :])
    pg = (ag * d_s[:, columns(j)]).astype(bf16)
    pg_s[:, columns(j)] = pg
    if own is not None:
        pgx_s[0:R, columns(own)] = pg


def block_grad(j, mod, pg_s, fc1, ni_s, sg_s, bo_s, blk_s, a1_s, a2_s, mod_out):
    blk = dot_nt(pg_s[...], fc1[columns(j), :])
    sp = 1.0 + mod[:, columns(j, W)].astype(f32)
    s0 = s1 = s2 = None
    for k in range(DRAWS):
        r = draw(k)
        n = ni_s[r, columns(j)]
        b = blk[r]
        bn = b * n
        g = b * sp
        blk_s[r, columns(j)] = g
        gn = g * n
        t1, t2 = g[:, :128] + g[:, 128:], gn[:, :128] + gn[:, 128:]
        a1_s[r, :] = t1 if j == 0 else a1_s[r, :] + t1
        a2_s[r, :] = t2 if j == 0 else a2_s[r, :] + t2
        s0 = b if s0 is None else s0 + b
        s1 = bn if s1 is None else s1 + bn
        t = sg_s[r, columns(j)] * bo_s[r, columns(j)]
        s2 = t if s2 is None else s2 + t
    mod_out[:, columns(j)] = s0
    mod_out[:, columns(j, W)] = s1
    mod_out[:, columns(j, 2 * W)] = s2


def input_grad(ri_s, ni_s, sg_s, blk_s, a1_s, a2_s, ib_s):
    for i in range(R // 32):
        r = slice(i * 32, (i + 1) * 32)
        m1 = jnp.sum(a1_s[r, :], axis=-1, keepdims=True) * (1.0 / W)
        m2 = jnp.sum(a2_s[r, :], axis=-1, keepdims=True) * (1.0 / W)
        v = sg_s[r, :] + ri_s[r, :] * (blk_s[r, :] - m1 - ni_s[r, :] * m2)
        ib_s[r, :] = v.astype(bf16)


MESH = pl.DeviceIdType.MESH
ORDER = (("y", "x", "z"), ("z", "y", "x"), ("x", "z", "y"))
HALF, PART, PIECE = W // 2, W // 6, 24
FACTOR = (ROWS * 128 // 2) ** -0.5
SEQ, HEAD, SPLIT = 16, 8, 4
GROUP = W // SEQ


def place():
    s, h = lax.axis_index("seq"), lax.axis_index("head")
    return {"y": lax.div(s, 4), "z": lax.rem(s, 4), "x": lax.div(h, 2)}, lax.rem(h, 2)


def away(pos, axis, d):
    out = dict(pos)
    out[axis] = lax.rem(pos[axis] + d, 4)
    return out


def device(pos, core):
    return (pos["y"] * 4 + pos["z"], pos["x"] * 2 + core)


def remote(src, dst, ssem, rsem, dev):
    return pltpu.make_async_remote_copy(
        src_ref=src, dst_ref=dst, send_sem=ssem, recv_sem=rsem, device_id=dev, device_id_type=MESH)


def peers(pos, core):
    s, h = lax.axis_index("seq"), lax.axis_index("head")
    out = [(lax.rem(s + d, SEQ), h) for d in range(1, SEQ)]
    out += [(s, lax.rem(h + d, HEAD)) for d in range(1, HEAD)]
    out += [device(away(pos, axis, d), 1 - core) for axis in ("y", "z") for d in (1, 2, 3)]
    return out


class Ring:
    def __init__(self, pos, core, axis, buf, got, ssem, rsem):
        self.a0 = pos[axis]
        self.buf, self.got = buf, got
        up, down = device(away(pos, axis, 1), core), device(away(pos, axis, 3), core)
        far, nxt, prv = (lax.rem(self.a0 + d, 4) for d in (2, 1, 3))
        self.nxt, self.prv = nxt, prv
        route = ((far, 0, up), (far, 1, down), (nxt, 1, up), (prv, 0, down), (nxt, 0, up), (prv, 1, down))
        self.copies = [
            remote(buf.at[k, half], got.at[i], ssem.at[i], rsem.at[i], dev) for i, (k, half, dev) in enumerate(route)]

    def start(self):
        self.start_far()
        self.start_near()

    def start_far(self):
        for c in self.copies[:2]:
            c.start()

    def start_near(self):
        for c in self.copies[2:4]:
            c.start()

    def relay(self):
        for i, k, half in ((0, self.nxt, 0), (1, self.prv, 1)):
            self.copies[i].wait_recv()
            total = self.buf[k, half].astype(f32) + self.got[i].astype(f32)
            self.buf[k, half] = total.astype(bf16)
            self.copies[4 + i].start()

    def finish(self):
        for i in (2, 3, 4, 5):
            self.copies[i].wait_recv()
        sums = []
        for half, i, j in ((0, 4, 3), (1, 2, 5)):
            sums.append(self.buf[self.a0, half].astype(f32) + self.got[i].astype(f32) + self.got[j].astype(f32))
        return sums

    def drain(self):
        for c in self.copies:
            c.wait_send()


class Direct:
    def __init__(self, pos, core, axis, buf, got, ssem, rsem):
        self.a0 = pos[axis]
        self.buf, self.got = buf, got
        self.copies = []
        for i, d in enumerate((2, 1, 3)):
            k = lax.rem(self.a0 + d, 4)
            for half in range(2):
                n = 2 * i + half
                self.copies.append(remote(buf.at[k, half], got.at[n], ssem.at[n], rsem.at[n], device(away(pos, axis, d), core)))

    def start(self):
        for c in self.copies:
            c.start()

    def relay(self):
        pass

    def finish(self):
        for c in self.copies:
            c.wait_recv()
        return [self.buf[self.a0, half].astype(f32) + self.got[half].astype(f32) + self.got[2 + half].astype(f32)
                + self.got[4 + half].astype(f32) for half in range(2)]

    def drain(self):
        for c in self.copies:
            c.wait_send()


def weight_own(left, right, acc):
    for y in range(2):
        acc[y] = dot_tn(left[0:R, y * 384:(y + 1) * 384], right[0:R, :])


def weight_parts(left, right, acc, out):
    prev = None
    for y in range(4):
        rows = slice(y * 384, (y + 1) * 384)
        if y < 2:
            g = acc[y] + dot_tn(left[R:2 * R, rows], right[R:2 * R, :])
        else:
            g = dot_tn(left[:, rows], right[...])
        g0, g1, g2 = (g[:, p * PART:(p + 1) * PART] for p in range(3))
        for x in range(4):
            v = jnp.concatenate([g0[(z * 4 + x) * PIECE:(z * 4 + x + 1) * PIECE] for z in range(4)], axis=0)
            out[0, y, x // 2, (x % 2) * 96:(x % 2 + 1) * 96] = v.astype(bf16)
        for z in range(4):
            out[1, z, y // 2, (y % 2) * 96:(y % 2 + 1) * 96] = g1[z * 96:(z + 1) * 96].astype(bf16)
        if y % 2 == 1:
            for z in range(4):
                for x in range(4):
                    at = (z * 4 + x) * PIECE
                    v = jnp.concatenate([prev[at:at + PIECE], g2[at:at + PIECE]], axis=0)
                    to = (z % 2) * 96 + (y // 2) * 48
                    out[2, x, z // 2, to:to + 48] = v.astype(bf16)
        prev = g2


def kernel(cnt, mod_in, lat_hbm, noise_hbm, times_hbm, inw_hbm, fc1_hbm, fc2_hbm, outw_hbm,
           mod_hbm, g_out, e_out,
           mod, lat, noise, times, inw, outw, noisy_s, st_s, ni_s, ri_s, d_s, bo_s, sg_s, ro_s, fin_s, pd_s, m_s, a1_s, a2_s,
           hx, bix, bg, bgx, pg, pgx, mod_out, fc1, fc2,
           acc, s1, r1, s2, r2, u_s, l_r, e_s, ec_s, ec_r, e2_s, e2_r, g_s, ee_s,
           load_sem, store_sem, pair_ss, pair_rs, ss1, rs1, ss2, rs2, ss3, rs3, ess, ers, fss, frs, out_sem):
    pos, core = place()
    seq, head = lax.axis_index("seq"), lax.axis_index("head")
    barrier = pltpu.get_barrier_semaphore()
    def load(n, src, dst):
        return [pltpu.make_async_copy(src.at[pl.ds(i * 384, 384)], dst.at[pl.ds(i * 384, 384)], load_sem.at[n, i])
                for i in range(4)]

    def wait(copies):
        for c in copies:
            c.wait()

    small = [pltpu.make_async_copy(src, dst, load_sem.at[2, i + 1]) for i, (src, dst) in enumerate(
        ((lat_hbm, lat), (noise_hbm, noise), (inw_hbm, inw), (outw_hbm, outw), (times_hbm, times)))]
    mod_load = pltpu.make_async_copy(mod_in, mod, load_sem.at[2, 0])
    fc1_load, fc2_load = load(0, fc1_hbm, fc1), load(1, fc2_hbm, fc2)
    for c in small + [mod_load] + fc1_load:
        c.start()
    met = peers(pos, core)
    for dev in met:
        pl.semaphore_signal(barrier, inc=1, device_id=dev, device_id_type=MESH)

    wait(small)
    make_noisy(lat, noise, times, noisy_s)
    stream(noisy_s, inw, st_s)
    mod_load.wait()
    norm_in(mod, st_s, ni_s, ri_s, bix)
    pl.semaphore_wait(barrier, len(met))

    other = device(pos, 1 - core)
    mine, theirs = core * 3, (1 - core) * 3
    half_at = pl.ds(pl.multiple_of((1 - core) * HALF, HALF), HALF)
    low, high = pl.ds(0, R), pl.ds(R, R)
    pair = {}

    def to_pair(name, n, src, dst):
        pair[name] = remote(src, dst, pair_ss.at[n], pair_rs.at[n], other)
        pair[name].start()

    rings1 = [[Ring(pos, core, ORDER[p][0], s1.at[m, p], r1.at[m, p], ss1.at[m, p], rs1.at[m, p])
               for p in range(3)] for m in range(2)]
    rings2 = [[Direct(pos, core, ORDER[p][1], s2.at[m, p], r2.at[m, p], ss2.at[m, p], rs2.at[m, p])
               for p in range(3)] for m in range(2)]
    stores = [pltpu.make_async_copy(mod_out.at[:, b * W:(b + 1) * W], mod_hbm.at[:, b * W:(b + 1) * W], store_sem.at[b])
              for b in range(3)]

    def each(m, name):
        for p in range(3):
            getattr(rings1[m][p], name)()

    def pass2(m, p):
        for hb, v in enumerate(rings1[m][p].finish()):
            v = v.astype(bf16)
            for b in range(2):
                for hc in range(2):
                    at = (b * 2 + hc) * 48
                    s2[m, p, 2 * hb + b, hc] = v[at:at + 48]
        rings2[m][p].start()

    def pass3(m, p):
        z = jnp.zeros((4, PART), f32)
        for hc, v in enumerate(rings2[m][p].finish()):
            for k in range(2):
                for c in range(2):
                    at = k * PIECE + c * 12
                    u_s[m, p, 2 * hc + k, c] = jnp.concatenate([v[at:at + 12], z], axis=0).astype(bf16)

    def finish_part(m, p):
        pass3(m, p)
        axis = ORDER[p][2]
        for rel in range(2):
            for d in (2, 1, 3, 0)[:3 + rel]:
                c = core if rel == 0 else 1 - core
                cp = remote(u_s.at[m, p, lax.rem(pos[axis] + d, 4), c], l_r.at[m, p, rel, d], ss3.at[m, p, rel, d],
                            rs3.at[m, p, rel, d], device(away(pos, axis, d), c))
                cp.start()
                last[m, p, rel, d] = cp

    out_copies = [pltpu.make_async_copy(g_s.at[pl.ds(16 * m, 16)], g_out.at[pl.ds(16 * m, 16)], out_sem.at[m]) for m in range(2)]
    out_copies.append(pltpu.make_async_copy(ee_s, e_out, out_sem.at[2]))

    def take(m):
        for p in range(3):
            for rel in range(2):
                v = u_s[m, p, pos[ORDER[p][2]], core].astype(f32) if rel == 0 else None
                for d in range(1 - rel, 4):
                    last[m, p, rel, d].wait_recv()
                    t = l_r[m, p, rel, d].astype(f32)
                    v = t if v is None else v + t
                g_s[m * 16:(m + 1) * 16, columns((mine if rel == 0 else theirs) + p)] = v * FACTOR
        out_copies[m].start()

    to_pair("bi", 0, bix.at[low], bix.at[high])
    wait(fc1_load)
    for c in fc2_load:
        c.start()
    fc1_fwd(bix, fc1, hx, d_s)
    to_pair("h", 1, hx.at[low], hx.at[high])
    wait(fc2_load)
    fc2_fwd(mod, hx, fc2, st_s, bo_s)
    for k in range(DRAWS):
        norm_out(k, st_s, ro_s, fin_s)
        predict(k, cnt, noise, fin_s, outw, pd_s, m_s)
    for i in range(3):
        stream_grad(theirs + i, None, mod, pd_s, outw, st_s, ro_s, m_s, sg_s, bg, bgx)
    to_pair("bg", 2, bg.at[:, half_at], bgx.at[high])
    for i in range(3):
        stream_grad(mine + i, i, mod, pd_s, outw, st_s, ro_s, m_s, sg_s, bg, bgx)
    weight_own(hx, bgx, acc)
    pair["h"].wait_recv()
    pair["bg"].wait_recv()
    weight_parts(hx, bgx, acc, s1.at[0])
    each(0, "start_far")
    each(0, "start_near")
    for i in range(3):
        pre_grad(theirs + i, None, bg, fc2, d_s, pg, pgx)
    to_pair("pg", 3, pg.at[:, half_at], pgx.at[high])
    for i in range(3):
        pre_grad(mine + i, i, bg, fc2, d_s, pg, pgx)
    weight_own(bix, pgx, acc)
    each(0, "relay")
    pair["bi"].wait_recv()
    pair["pg"].wait_recv()
    weight_parts(bix, pgx, acc, s1.at[1])
    each(1, "start_far")
    each(1, "start_near")
    e_s[C:2 * C, 0:W] = dot(pd_s[...], fin_s[...])
    e_s[:, W:] = jnp.zeros((2 * C, 128), f32)
    for j in range(6):
        block_grad(j, mod, pg, fc1, ni_s, sg_s, bo_s, st_s, a1_s, a2_s, mod_out)
    for c in stores:
        c.start()
    for p in range(3):
        pass2(0, p)
    input_grad(ri_s, ni_s, sg_s, st_s, a1_s, a2_s, fin_s)
    e_s[0:C, 0:W] = dot(noisy_s[...], fin_s[...])
    for k in range(SEQ):
        ec_s[k] = e_s[:, GROUP * k:GROUP * k + 128].astype(bf16)
    each(1, "relay")
    edge1 = [remote(ec_s.at[lax.rem(seq + d, SEQ)], ec_r.at[d - 1], ess.at[d - 1], ers.at[d - 1],
                    (lax.rem(seq + d, SEQ), head)) for d in range(1, SEQ)]
    for c in edge1:
        c.start()
    for p in range(3):
        pass2(1, p)
    last = {}
    tot = ec_s[seq].astype(f32)
    for i, c in enumerate(edge1):
        c.wait_recv()
        tot = tot + ec_r[i].astype(f32)
    e2_s[...] = tot
    edge2 = [remote(e2_s, e2_r.at[d - 1], fss.at[d - 1], frs.at[d - 1], (seq, lax.rem(head + d, HEAD)))
             for d in range(1, HEAD)]
    for c in edge2:
        c.start()
    for p in range(3):
        finish_part(0, p)
    for p in range(3):
        finish_part(1, p)
    take(0)
    for i, c in enumerate(edge2):
        c.wait_recv()
        tot = tot + e2_r[i]
    ee_s[...] = pltpu.roll(tot * FACTOR, lax.rem(128 - 12 * head, 128), 1)
    out_copies[2].start()
    take(1)
    for m in range(2):
        for p in range(3):
            rings1[m][p].drain()
            rings2[m][p].drain()
    for c in list(pair.values()) + edge1 + edge2 + list(last.values()):
        c.wait_send()
    for c in stores + out_copies:
        c.wait()


def fused_call(mod, lat, noise, times, cnt, inw, fc1, fc2, outw):
    v = pl.BlockSpec(memory_space=pltpu.VMEM)
    hbm = pl.BlockSpec(memory_space=pl.ANY)
    O = jax.ShapeDtypeStruct
    V = pltpu.VMEM
    D = pltpu.SemaphoreType.DMA
    big = V((R, W), bf16)
    two = V((2 * R, W), bf16)
    half = V((2 * R, HALF), bf16)
    return pl.pallas_call(
        kernel,
        out_shape=[O((ROWS, 3 * W), f32), O((32, W), f32), O((2 * C, 128), f32)],
        in_specs=[pl.BlockSpec(memory_space=pltpu.SMEM), hbm, hbm, hbm, hbm, hbm, hbm, hbm, hbm],
        out_specs=[hbm, hbm, hbm],
        scratch_shapes=[
            V((ROWS, 3 * W), bf16), V((C, ROWS), bf16), V((DRAWS * C, ROWS), bf16), V((DRAWS, ROWS), bf16), V((C, W), bf16), V((C, W), bf16), V((C, R), bf16), V((R, W), f32), V((R, W), f32), V((R, 1), f32), V((R, W), f32),
            V((R, W), f32), V((R, W), f32), V((R, 1), f32), big, V((C, R), bf16), V((R, 8), f32), V((R, 128), f32), V((R, 128), f32),
            two, two, big, half, big, half, V((ROWS, 3 * W), f32), V((W, W), bf16), V((W, W), bf16),
            V((2, 384, HALF), f32), V((2, 3, 4, 2, 192, PART), bf16), V((2, 3, 6, 192, PART), bf16),
            V((2, 3, 4, 2, 48, PART), bf16), V((2, 3, 6, 48, PART), bf16),
            V((2, 3, 4, 2, 16, PART), bf16), V((2, 3, 2, 4, 16, PART), bf16),
            V((2 * C, W + 128), f32), V((SEQ, 2 * C, 128), bf16), V((SEQ - 1, 2 * C, 128), bf16),
            V((2 * C, 128), f32), V((HEAD - 1, 2 * C, 128), f32), V((32, W), f32), V((2 * C, 128), f32),
            D((3, 6)), D((3,)), D((4,)), D((4,)), D((2, 3, 6)), D((2, 3, 6)), D((2, 3, 6)), D((2, 3, 6)),
            D((2, 3, 2, 4)), D((2, 3, 2, 4)), D((SEQ - 1,)), D((SEQ - 1,)), D((HEAD - 1,)), D((HEAD - 1,)), D((3,)),
        ],
        compiler_params=pltpu.CompilerParams(
            collective_id=0, has_side_effects=True, vmem_limit_bytes=62 * 1024 * 1024),
        cost_estimate=pl.CostEstimate(flops=12 * R * W * W, bytes_accessed=20_000_000, transcendentals=R * W),
    )(cnt, mod, lat.T, noise.T, times.T, inw, fc1, fc2, outw)


def split_kernel(mod_hbm, g_hbm, e_hbm, mod_out, fc1_out, fc2_out, in_out, out_out,
                 buf, g, e, fc1_s, fc2_s, in_s, out_s, in_sem, out_sem):
    n = ROWS // SPLIT
    parts = [pl.ds(i * n, n) for i in range(SPLIT)]
    into = [pltpu.make_async_copy(src, dst, in_sem.at[SPLIT + i]) for i, (src, dst) in enumerate(((g_hbm, g), (e_hbm, e)))]
    into += [pltpu.make_async_copy(mod_hbm.at[r], buf.at[r], in_sem.at[i]) for i, r in enumerate(parts)]
    small = ((fc1_s, fc1_out), (fc2_s, fc2_out), (in_s, in_out), (out_s, out_out))
    out = [pltpu.make_async_copy(src, dst, out_sem.at[SPLIT + i]) for i, (src, dst) in enumerate(small)]
    out += [pltpu.make_async_copy(buf.at[r], mod_out.at[r], out_sem.at[i]) for i, r in enumerate(parts)]
    for c in into:
        c.start()
    into[0].wait()
    into[1].wait()
    fc2_s[...] = g[0:12]
    fc1_s[...] = g[16:28]
    in_s[...] = e[0:C, 0:12]
    out_s[...] = e[C:2 * C, 0:12]
    for c in out[:4]:
        c.start()
    for a, b in zip(into[2:], out[4:]):
        a.wait()
        b.start()
    for c in out:
        c.wait()


def split_call(mod_grad, g, e):
    hbm = pl.BlockSpec(memory_space=pl.ANY)
    O = jax.ShapeDtypeStruct
    V = pltpu.VMEM
    return pl.pallas_call(
        split_kernel,
        out_shape=[O((ROWS, 3 * W), f32), O((12, W), f32), O((12, W), f32), O((C, 12), f32), O((C, 12), f32)],
        in_specs=[hbm] * 3,
        out_specs=[hbm] * 5,
        scratch_shapes=[V((ROWS, 3 * W), f32), V((32, W), f32), V((2 * C, 128), f32), V((12, W), f32), V((12, W), f32),
                        V((C, 12), f32), V((C, 12), f32),
                        pltpu.SemaphoreType.DMA((SPLIT + 2,)), pltpu.SemaphoreType.DMA((SPLIT + 4,))],
        compiler_params=pltpu.CompilerParams(vmem_limit_bytes=60 * 1024 * 1024),
    )(mod_grad, g, e)


def body(modulation, latents, noise, times, image_rows, in_weight, fc1_weight, fc2_weight, out_weight):
    mod_grad, g, e = fused_call(
        modulation, latents, noise, times, image_rows, in_weight, fc1_weight, fc2_weight, out_weight)
    return tuple(split_call(mod_grad, g, e))


def solution(mesh):
    rows = P(("seq", "head"), None)
    cols = P(None, ("seq", "head"))
    return jax.shard_map(
        body, mesh=mesh, in_specs=(rows, rows, rows, rows, P(("seq", "head")), P(), P(), P(), P()),
        out_specs=(rows, rows, rows, cols, cols), check_vma=False)
```
